32 devices in a mesh: dp: 4 (over y, x), ctx: 8 (over z, core).
Axes of the slice: x: 2, y: 2, z: 4, core: 2. Of those that a mesh axis runs over, the one named last changes fastest.
Arguments:
- hidden_in: bfloat16 [4, 1024, 4096], P('dp', 'ctx'), may hold values from -6 to 6
- write_weight: bfloat16 [4096, 128], P(('dp', 'ctx')), may hold values from -0.09375 to 0.09375
- shard_scale: float32 [32], P(('dp', 'ctx')), may hold values from 0.5 to 2
- inner_acts: bfloat16 [4, 1024, 4096], P('dp', 'ctx'), may hold values from -6 to 6
- read_proj: bfloat16 [4, 1024, 128], P('dp', 'ctx'), may hold values from -0.13183594 to 0.13183594
- step_size: float32 [4, 64, 1024], P('dp', None, 'ctx'), may hold values from 0.1 to 1
- log_decay: float32 [4, 64, 1024], P('dp', None, 'ctx'), may hold values from -2 to 0
- grad_fwd: bfloat16 [4, 1024, 4096], P('dp', 'ctx'), may hold values from -1.5 to 1.5
- grad_rev: bfloat16 [4, 1024, 4096], P('dp', 'ctx'), may hold values from -1.5 to 1.5
Outputs:
- grad_inner: bfloat16 [4, 1024, 4096], P('dp', 'ctx')
- grad_hidden: bfloat16 [4, 1024, 4096], P('dp', 'ctx')
- grad_weight: float32 [4096, 128], P(('dp', 'ctx'))
The draws below stay inside these ranges and needn't reach their ends.
All inputs are finite; a program needn't handle non-finite values.
Results may differ from the reference program's by a relative error of at most 0.0064.
Values may be sent and summed in bfloat16 or wider, within the bound.
No kernel may reach another device: no remote copies, remote signals or barrier semaphores. Data moves between devices by JAX's collectives and lax.ppermute only.
A program may use at most 256 MiB of HBM per device.

```python
import math
import jax
import jax.numpy as jnp
from jax import lax

D = 4096
HALF_HEADS = 64
STATE = 128
BLOCK = 128
TOK_DEV = 128
E = 4096
SEQUENCE_LENGTH = 1024
BATCH_SEQUENCES = 4
SHARDS = 32


def draw_log_decay(key, part):
    random_subkeys = jax.random.split(key, 5)
    fast_limit = 4
    fast_heads = jax.random.randint(random_subkeys[0], (BATCH_SEQUENCES, HALF_HEADS, 1), 0, 8) < fast_limit
    baseline_rate = jnp.where(fast_heads, 0.08, 0.3 / SEQUENCE_LENGTH)
    jaggedness = jnp.exp(jax.random.uniform(random_subkeys[1], (BATCH_SEQUENCES, HALF_HEADS, SEQUENCE_LENGTH), minval=-0.7, maxval=0.7))
    span_count = SEQUENCE_LENGTH // TOK_DEV
    block_factor_scale = jnp.exp(jax.random.uniform(random_subkeys[2], (BATCH_SEQUENCES, HALF_HEADS, span_count, 1), minval=-0.7, maxval=0.7))
    block_factor_scale = jnp.broadcast_to(block_factor_scale, (BATCH_SEQUENCES, HALF_HEADS, span_count, TOK_DEV)).reshape(BATCH_SEQUENCES, HALF_HEADS, SEQUENCE_LENGTH)
    spike_locations = jax.random.randint(random_subkeys[3], (BATCH_SEQUENCES, HALF_HEADS, 2, 1), 0, SEQUENCE_LENGTH)
    spike_decrements = jnp.log(jax.random.uniform(random_subkeys[4], (BATCH_SEQUENCES, HALF_HEADS, 2, 1), minval=0.5, maxval=0.8))
    position_indices = jnp.arange(SEQUENCE_LENGTH)[None, None, None, :]
    spike_events = jnp.sum(jnp.where(position_indices == spike_locations, spike_decrements, 0.0), axis=2)
    return (-baseline_rate * jaggedness * block_factor_scale + spike_events).astype(jnp.float32)


def block_levels(rng, extent, cuts, least, largest):
    level, own = 1.0, jax.random.fold_in(rng, 6)
    for position, blocks in cuts:
        steps = jnp.exp(jax.random.uniform(jax.random.fold_in(own, position), (blocks,), jnp.float32, least / len(cuts), largest / len(cuts)))
        level = level * jnp.repeat(steps, extent[position] // blocks).reshape([-1 if axis == position else 1 for axis in range(len(extent))])
    return level


def noise(key, shape, spread, most, cuts=(), held_as=jnp.bfloat16):
    drawn = spread * jax.random.normal(key, shape, jnp.float32)
    if cuts:
        drawn = drawn * block_levels(key, shape, cuts, -0.22, 0.18)
    return jnp.clip(drawn, -most, most).astype(held_as)


def setup_inputs(seed: int = 0) -> dict:
    arg_keys = jax.random.split(jax.random.key(seed), 10)
    return {
        "hidden_in": noise(arg_keys[0], (BATCH_SEQUENCES, SEQUENCE_LENGTH, D), 1.0, 6.0, ((0, 4), (1, 8))),
        "write_weight": noise(arg_keys[1], (D, STATE), D ** -0.5, 0.09375, ((0, 32),)),
        "shard_scale": jnp.clip(jnp.exp(math.log(2.0) - 1.3862944 * jax.random.uniform(arg_keys[2], (SHARDS,), jnp.float32) ** block_levels(arg_keys[2], (SHARDS,), ((0, 32),), -0.2, 0.2)), 0.5, 2.0),
        "inner_acts": noise(arg_keys[3], (BATCH_SEQUENCES, SEQUENCE_LENGTH, E), 1.0, 6.0, ((0, 4), (1, 8))),
        "read_proj": noise(arg_keys[4], (BATCH_SEQUENCES, SEQUENCE_LENGTH, STATE), (0.25 / STATE ** 0.5), 0.13183594, ((0, 4), (1, 8))),
        "step_size": jnp.clip(jnp.exp(math.log(1.0) - 2.3025851 * jax.random.uniform(arg_keys[5], (BATCH_SEQUENCES, HALF_HEADS, SEQUENCE_LENGTH), jnp.float32) ** block_levels(arg_keys[5], (BATCH_SEQUENCES, HALF_HEADS, SEQUENCE_LENGTH), ((0, 4), (2, 8)), -0.2, 0.2)), 0.1, 1.0),
        "log_decay": draw_log_decay(jax.random.fold_in(arg_keys[9], 71), 0),
        "grad_fwd": noise(arg_keys[7], (BATCH_SEQUENCES, SEQUENCE_LENGTH, E), 0.25, 1.5, ((0, 4), (1, 8))),
        "grad_rev": noise(arg_keys[8], (BATCH_SEQUENCES, SEQUENCE_LENGTH, E), 0.25, 1.5, ((0, 4), (1, 8))),
    }


masked_low = -1e30


def decay_state(decays, state_mat):
    head_count = decays.shape[0]
    shaped = state_mat.reshape(state_mat.shape[0], head_count, state_mat.shape[1] // head_count)
    return (shaped * decays[None, :, None]).reshape(state_mat.shape)


def block_cums(decay_rows):
    local_cum = jnp.cumsum(decay_rows, axis=1)
    return local_cum, local_cum - decay_rows


def block_summary(read_rows, decay_rows, fwd_rows, back_rows):
    local_cum, local_excl = block_cums(decay_rows)
    block_end = local_cum[:, -1:]
    head_count = decay_rows.shape[0]
    row_count = fwd_rows.shape[0]
    col_count = fwd_rows.shape[1]
    fwd_weight = jnp.exp(local_cum).T
    back_weight = jnp.exp(block_end - local_excl).T
    fwd_scaled = (fwd_rows.astype(jnp.float32).reshape(row_count, head_count, col_count // head_count) * fwd_weight[:, :, None]).reshape(row_count, col_count).astype(jnp.bfloat16)
    back_scaled = (back_rows.astype(jnp.float32).reshape(row_count, head_count, col_count // head_count) * back_weight[:, :, None]).reshape(row_count, col_count).astype(jnp.bfloat16)
    right_part = jnp.dot(read_rows.T, fwd_scaled, preferred_element_type=jnp.float32)
    left_part = jnp.dot(read_rows.T, back_scaled, preferred_element_type=jnp.float32)
    return jnp.exp(block_end[:, 0]), right_part, left_part


def block_outputs(inner_rows, read_rows, write_rows, step_rows, decay_rows, fwd_rows, back_rows, right_in, left_in):
    local_cum, local_excl = block_cums(decay_rows)
    block_end = local_cum[:, -1:]
    row_count = inner_rows.shape[0]
    head_count = step_rows.shape[0]
    col_count = inner_rows.shape[1]
    head_dim = col_count // head_count
    kernel = jnp.dot(write_rows, read_rows.T, preferred_element_type=jnp.float32)
    position_indices = jnp.arange(row_count)
    upper_mask = position_indices[None, :] >= position_indices[:, None]
    lower_mask = position_indices[None, :] <= position_indices[:, None]
    fwd_decay = jnp.exp(jnp.where(upper_mask[None], local_cum[:, None, :] - local_cum[:, :, None], masked_low))
    rev_decay = jnp.exp(jnp.where(lower_mask[None], local_excl[:, :, None] - local_excl[:, None, :], masked_low))
    fwd_mix = (fwd_decay * kernel[None]).astype(jnp.bfloat16)
    rev_mix = (rev_decay * kernel[None]).astype(jnp.bfloat16)
    fwd_heads = fwd_rows.astype(jnp.float32).reshape(row_count, head_count, head_dim)
    back_heads = back_rows.astype(jnp.float32).reshape(row_count, head_count, head_dim)
    inner_heads = inner_rows.astype(jnp.float32).reshape(row_count, head_count, head_dim)
    intra_sum = jnp.einsum("hst,thp->shp", fwd_mix.astype(jnp.float32), fwd_heads) + jnp.einsum("hst,thp->shp", rev_mix.astype(jnp.float32), back_heads)
    write_float = write_rows.astype(jnp.float32)
    right_term = jnp.dot(write_float, right_in, precision=lax.Precision.HIGHEST).reshape(row_count, head_count, head_dim)
    left_term = jnp.dot(write_float, left_in, precision=lax.Precision.HIGHEST).reshape(row_count, head_count, head_dim)
    fwd_edge = jnp.exp(block_end - local_cum).T
    back_edge = jnp.exp(local_excl).T
    step_cols = step_rows.T
    combined = intra_sum + fwd_edge[:, :, None] * right_term + back_edge[:, :, None] * left_term
    grad_block = (step_cols[:, :, None] * combined).reshape(row_count, col_count).astype(jnp.bfloat16)
    fwd_dots = jnp.einsum("thp,shp->hst", fwd_heads, inner_heads)
    back_dots = jnp.einsum("thp,shp->hst", back_heads, inner_heads)
    mixed_weights = jnp.sum(step_rows[:, :, None] * (fwd_decay * fwd_dots + rev_decay * back_dots), axis=0).astype(jnp.bfloat16)
    intra_write = jnp.dot(mixed_weights, read_rows, preferred_element_type=jnp.float32)
    fwd_inner = (inner_heads * (step_cols * fwd_edge)[:, :, None]).reshape(row_count, col_count)
    back_inner = (inner_heads * (step_cols * back_edge)[:, :, None]).reshape(row_count, col_count)
    edge_write = jnp.dot(fwd_inner, right_in.T, precision=lax.Precision.HIGHEST) + jnp.dot(back_inner, left_in.T, precision=lax.Precision.HIGHEST)
    write_block = (intra_write + edge_write).astype(jnp.bfloat16)
    return grad_block, write_block


def reference(hidden_in, write_weight, shard_scale, inner_acts, read_proj, step_size, log_decay, grad_fwd, grad_rev):
    shard_rows = D // SHARDS
    weight_eff = (write_weight.astype(jnp.float32) * jnp.repeat(shard_scale, shard_rows)[:, None]).astype(jnp.bfloat16)
    block_count = SEQUENCE_LENGTH // BLOCK

    def split_rows(array):
        return array.reshape(block_count, BLOCK, array.shape[-1])

    def split_cols(array):
        return array.reshape(array.shape[0], block_count, BLOCK).transpose(1, 0, 2)

    def carry_step(state_mat, block_item):
        factor, part_state = block_item
        return part_state + decay_state(factor, state_mat), state_mat

    def one_sequence(accumulated, seq_item):
        hidden, inner_seq, read_seq, step_seq, decay_seq, fwd_seq, rev_seq = seq_item
        write_seq = jnp.dot(hidden, weight_eff, preferred_element_type=jnp.float32).astype(jnp.bfloat16)
        back_seq = rev_seq[::-1]
        read_blocks = split_rows(read_seq)
        decay_blocks = split_cols(decay_seq)
        fwd_blocks = split_rows(fwd_seq)
        back_blocks = split_rows(back_seq)
        decays, right_parts, left_parts = lax.map(lambda block_item: block_summary(*block_item), (read_blocks, decay_blocks, fwd_blocks, back_blocks))
        zero_state = jnp.zeros((STATE, E), jnp.float32)
        ignored, right_ins = lax.scan(carry_step, zero_state, (decays, right_parts), reverse=True)
        ignored, left_ins = lax.scan(carry_step, zero_state, (decays, left_parts))
        grad_blocks, write_blocks = lax.map(lambda block_item: block_outputs(*block_item), (split_rows(inner_seq), read_blocks, split_rows(write_seq), split_cols(step_seq), decay_blocks, fwd_blocks, back_blocks, right_ins, left_ins))
        grad_write = write_blocks.reshape(SEQUENCE_LENGTH, STATE)
        grad_hid = jnp.dot(grad_write, weight_eff.T, preferred_element_type=jnp.float32).astype(jnp.bfloat16)
        accumulated = accumulated + jnp.dot(hidden.T, grad_write, preferred_element_type=jnp.float32)
        return accumulated, (grad_blocks.reshape(SEQUENCE_LENGTH, E), grad_hid)

    accumulated, outputs = lax.scan(one_sequence, jnp.zeros((D, STATE), jnp.float32), (hidden_in, inner_acts, read_proj, step_size, log_decay, grad_fwd, grad_rev))
    return outputs[0], outputs[1], accumulated / (BATCH_SEQUENCES * SEQUENCE_LENGTH)
```

```python
import functools

import jax
import jax.numpy as jnp
from jax import lax
from jax.experimental import pallas as pl
from jax.experimental.pallas import tpu as pltpu
from jax.sharding import PartitionSpec as P

BLOCK = 128
LANES = 128
GROUP = 8
LOG2E = 1.4426950408889634
LOW = -1e30
EXACT = lax.Precision.HIGHEST
VMEM_BYTES = 48 * 1024 * 1024

f32 = jnp.float32
bf16 = jnp.bfloat16

CUM2, EXCLR2, W_FWD, W_BACK, FWD_EDGE, BACK_EDGE, STEP = range(7)
C_MIX_FWD, C_MIX_BACK, C_CUM2, C_EXCL2 = range(4)


def local_call(body, out_shape, scratch=()):
    many = isinstance(out_shape, (list, tuple))
    vmem = pl.BlockSpec(memory_space=pltpu.VMEM)
    return pl.pallas_call(
        body,
        out_shape=out_shape,
        out_specs=[vmem] * len(out_shape) if many else vmem,
        scratch_shapes=list(scratch),
        compiler_params=pltpu.CompilerParams(vmem_limit_bytes=VMEM_BYTES),
    )


def iotas(shape):
    return lax.broadcasted_iota(jnp.int32, shape, 0), lax.broadcasted_iota(jnp.int32, shape, 1)


def dot_nt(a, b):
    return lax.dot_general(a, b, (((1,), (1,)), ((), ())), preferred_element_type=f32)


def dot_tn(a, b):
    return lax.dot_general(a, b, (((0,), (0,)), ((), ())), preferred_element_type=f32)


def spread(rows, width):
    high = rows.astype(bf16).astype(f32)
    both = jnp.concatenate([high, rows - high], axis=0).astype(bf16)
    r, c = iotas((2 * GROUP, GROUP * width))
    pick = (r % GROUP == c // width).astype(f32).astype(bf16)
    return dot_tn(both, pick)


def tables_kernel(read_ref, decay_ref, step_ref, readr_ref, rows_ref, cols_ref):
    decay = decay_ref[...]
    heads, n = decay.shape
    r, c = iotas((n, n))
    upto = (r <= c).astype(f32)
    flip = (r + c == n - 1).astype(f32)
    readr_ref[...] = jnp.dot(
        flip.astype(bf16), read_ref[...], preferred_element_type=f32
    ).astype(bf16)
    cum = jnp.dot(decay, upto, precision=EXACT, preferred_element_type=f32)
    decay_r = jnp.dot(decay, flip, precision=EXACT, preferred_element_type=f32)
    cum_r = jnp.dot(decay_r, upto, precision=EXACT, preferred_element_type=f32)
    end = cum[:, n - 1 :]
    excl = cum - decay
    step = step_ref[...]
    log_step = jnp.log(step) * LOG2E
    cum2 = cum * LOG2E
    excl2 = excl * LOG2E
    rows_ref[CUM2] = cum2
    rows_ref[EXCLR2] = (end - cum_r) * LOG2E
    rows_ref[W_FWD] = jnp.exp(cum)
    rows_ref[W_BACK] = jnp.exp(cum_r)
    rows_ref[FWD_EDGE] = step * jnp.exp(end - cum)
    rows_ref[BACK_EDGE] = step * jnp.exp(excl)
    rows_ref[STEP] = step
    planes = (cum2 - log_step, excl2 + log_step, cum2, excl2)
    rest = jnp.zeros((LANES - GROUP * len(planes), n), f32)
    for g in range(heads // GROUP):
        part = [p[g * GROUP : (g + 1) * GROUP] for p in planes]
        cols_ref[g] = jnp.concatenate(part + [rest], axis=0).T


def part_kernel(g_ref, read_ref, w_ref, out_ref):
    heads, n = w_ref.shape
    width = g_ref.shape[1] // heads
    step = GROUP * width
    read_t = read_ref[...].astype(f32).T.astype(bf16)
    state = read_t.shape[0]

    def one(g, carry):
        at = pl.multiple_of(g * step, step)
        scale = spread(w_ref[pl.ds(pl.multiple_of(g * GROUP, GROUP), GROUP)], width)
        scaled = (g_ref[:, pl.ds(at, step)].astype(f32) * scale).astype(bf16)
        part = jnp.dot(read_t, scaled, preferred_element_type=f32)
        out_ref[0:state, pl.ds(at, step)] = part.astype(bf16)
        last = scale[n - 1 :]
        high = last.astype(bf16).astype(f32)
        r, _ = iotas((16, step))
        tail = jnp.where(r == 0, high, jnp.where(r == 1, last - high, 0.0))
        out_ref[state : state + 16, pl.ds(at, step)] = tail.astype(bf16)
        return carry

    lax.fori_loop(0, heads // GROUP, one, 0)


def mix_kernel(fwd, inner_ref, g_ref, row_ref, cols_ref, out_ref):
    heads, n = row_ref.shape
    width = g_ref.shape[1] // heads
    step = GROUP * width
    s, t = iotas((n, n))
    keep = (t >= s) if fwd else (t + s >= n - 1)
    low_half = t < width

    def one(g, acc):
        at = pl.multiple_of(g * step, step)
        rows = row_ref[pl.ds(pl.multiple_of(g * GROUP, GROUP), GROUP)]
        cols = cols_ref[g]
        for pair in range(GROUP // 2):
            here = pl.ds(at + pair * LANES, LANES)
            inner = inner_ref[:, here].astype(f32)
            halves = jnp.concatenate(
                [jnp.where(low_half, inner, 0.0), jnp.where(low_half, 0.0, inner)], axis=0
            ).astype(bf16)
            dots = dot_nt(halves, g_ref[:, here])
            for j in range(2):
                h = 2 * pair + j
                row = rows[h : h + 1]
                if fwd:
                    k = C_MIX_FWD * GROUP + h
                    power = row - cols[:, k : k + 1]
                else:
                    k = C_MIX_BACK * GROUP + h
                    power = cols[:, k : k + 1] - row
                decay = jnp.exp2(jnp.where(keep, power, LOW))
                acc = acc + decay * dots[j * n : (j + 1) * n]
        return acc

    out_ref[...] = lax.fori_loop(0, heads // GROUP, one, jnp.zeros((n, n), f32))


def write_kernel(
    inner_ref, right_ref, left_ref, rows_ref, mixf_ref, mixb_ref, read_ref, readr_ref, out_ref
):
    _, heads, n = rows_ref.shape
    width = inner_ref.shape[1] // heads
    step = GROUP * width

    def one(g, acc):
        at = pl.multiple_of(g * step, step)
        own = pl.ds(pl.multiple_of(g * GROUP, GROUP), GROUP)
        inner = inner_ref[:, pl.ds(at, step)].astype(f32)
        fwd = (inner * spread(rows_ref[FWD_EDGE, own], width)).astype(bf16)
        back = (inner * spread(rows_ref[BACK_EDGE, own], width)).astype(bf16)
        return (
            acc
            + dot_nt(fwd, right_ref[:, pl.ds(at, step)])
            + dot_nt(back, left_ref[:, pl.ds(at, step)])
        )

    acc = jnp.dot(mixf_ref[...].astype(bf16), read_ref[...], preferred_element_type=f32)
    acc = acc + jnp.dot(mixb_ref[...].astype(bf16), readr_ref[...], preferred_element_type=f32)
    out_ref[...] = lax.fori_loop(0, heads // GROUP, one, acc).astype(bf16)


def inner_kernel(
    gf_ref, gb_ref, right_ref, left_ref, rows_ref, cols_ref, write_ref, read_ref, readr_ref, out_ref
):
    _, heads, n = rows_ref.shape
    width = gf_ref.shape[1] // heads
    step = GROUP * width
    write = write_ref[...]
    kernel_f = dot_nt(write, read_ref[...])
    kernel_b = dot_nt(write, readr_ref[...])
    s, t = iotas((n, n))
    low_half = t < width

    def one(g, carry):
        at = pl.multiple_of(g * step, step)
        own = pl.ds(pl.multiple_of(g * GROUP, GROUP), GROUP)
        cols = cols_ref[g]
        cum2 = rows_ref[CUM2, own]
        exclr2 = rows_ref[EXCLR2, own]
        step_e = spread(rows_ref[STEP, own], width)
        edges = spread(rows_ref[FWD_EDGE, own], width) * jnp.dot(
            write, right_ref[:, pl.ds(at, step)], preferred_element_type=f32
        )
        edges = edges + spread(rows_ref[BACK_EDGE, own], width) * jnp.dot(
            write, left_ref[:, pl.ds(at, step)], preferred_element_type=f32
        )
        for pair in range(GROUP // 2):
            mixes = []
            for j in range(2):
                h = 2 * pair + j
                kf = C_CUM2 * GROUP + h
                kb = C_EXCL2 * GROUP + h
                pf = cum2[h : h + 1] - cols[:, kf : kf + 1]
                pb = cols[:, kb : kb + 1] - exclr2[h : h + 1]
                mf = jnp.exp2(jnp.where(t >= s, pf, LOW)) * kernel_f
                mb = jnp.exp2(jnp.where(t + s >= n - 1, pb, LOW)) * kernel_b
                mixes.append(jnp.concatenate([mf, mb], axis=1))
            here = pl.ds(at + pair * LANES, LANES)
            both = jnp.concatenate([gf_ref[:, here], gb_ref[:, here]], axis=0)
            got = jnp.dot(
                jnp.concatenate(mixes, axis=0).astype(bf16), both, preferred_element_type=f32
            )
            intra = jnp.where(low_half, got[:n], got[n:])
            mine = slice(pair * LANES, (pair + 1) * LANES)
            out_ref[:, here] = (step_e[:, mine] * intra + edges[:, mine]).astype(bf16)
        return carry

    lax.fori_loop(0, heads // GROUP, one, 0)


def xor_pairs(count, k):
    return [(i, i ^ k) for i in range(count)]


def chip_states(part, ctx_count, core, upward):
    state = part.shape[0] - 16
    cols = part.shape[1]
    half = cols // 2
    chips = ctx_count // 2
    other = lax.ppermute(part, "ctx", xor_pairs(ctx_count, 1))
    first = core == (0 if upward else 1)

    def split(array):
        mine = lax.dynamic_slice_in_dim(array, core * half, half, 1).astype(f32)
        return mine[:state], mine[state : state + 1] + mine[state + 1 : state + 2]

    own_term, own_decay = split(part)
    other_term, other_decay = split(other)
    later_decay = jnp.where(first, other_decay, own_decay)
    both = jnp.where(first, other_term, own_term) + later_decay * jnp.where(
        first, own_term, other_term
    )
    both_decay = own_decay * other_decay
    entering = jnp.zeros((state, half), bf16)
    for hop in range(chips - 1):
        if upward:
            source, target = hop, hop + 1
        else:
            source, target = chips - 1 - hop, chips - 2 - hop
        if hop:
            leaving = (both + both_decay * entering.astype(f32)).astype(bf16)
        else:
            leaving = both.astype(bf16)
        pairs = [(2 * source + i, 2 * target + i) for i in range(2)]
        entering = entering + lax.ppermute(leaving, "ctx", pairs)
    swapped = lax.ppermute(entering, "ctx", xor_pairs(ctx_count, 1))
    whole = jnp.where(
        core == 0,
        jnp.concatenate([entering, swapped], axis=1),
        jnp.concatenate([swapped, entering], axis=1),
    )
    decay = other[state : state + 1].astype(f32) + other[state + 1 : state + 2].astype(f32)
    second = other[:state].astype(f32) + decay * whole.astype(f32)
    return jnp.where(first, whole, second.astype(bf16))


def shards(
    hidden_in,
    write_weight,
    shard_scale,
    inner_acts,
    read_proj,
    step_size,
    log_decay,
    grad_fwd,
    grad_rev,
):
    ctx_count = lax.axis_size("ctx")
    dp_count = lax.axis_size("dp")
    ctx = lax.axis_index("ctx")
    dp = lax.axis_index("dp")
    core = ctx % 2
    hidden = hidden_in[0]
    inner = inner_acts[0]
    read = read_proj[0]
    step = step_size[0]
    decay = log_decay[0]
    gf = grad_fwd[0]
    n, width = inner.shape
    heads = decay.shape[0]
    state = read.shape[1]
    rows_all = hidden.shape[1]

    gb = lax.ppermute(grad_rev[0], "ctx", [(i, ctx_count - 1 - i) for i in range(ctx_count)])

    local_weight = (write_weight.astype(f32) * shard_scale[0]).astype(bf16)
    weight = lax.all_gather(local_weight, ("dp", "ctx"), axis=0, tiled=True)

    share = rows_all // dp_count

    def of_dp(array, k):
        return lax.dynamic_slice_in_dim(array, (dp ^ k) * share, share, 1)

    hidden_parts = [of_dp(hidden, 0)] + [
        lax.ppermute(of_dp(hidden, k), "dp", xor_pairs(dp_count, k)) for k in range(1, dp_count)
    ]

    sds = jax.ShapeDtypeStruct
    read_r, rows, cols = local_call(
        tables_kernel,
        [
            sds((n, state), bf16),
            sds((7, heads, n), f32),
            sds((heads // GROUP, n, LANES), f32),
        ],
    )(read, decay, step)

    part_call = local_call(part_kernel, sds((state + 16, width), bf16))
    right_part = part_call(gf, read, rows[W_FWD])
    right_in = chip_states(right_part, ctx_count, core, False)
    mix_f = local_call(functools.partial(mix_kernel, True), sds((n, n), f32))(
        inner, gf, rows[CUM2], cols
    )
    left_part = part_call(gb, read_r, rows[W_BACK])
    left_in = chip_states(left_part, ctx_count, core, True)
    mix_b = local_call(functools.partial(mix_kernel, False), sds((n, n), f32))(
        inner, gb, rows[EXCLR2], cols
    )
    grad_write = local_call(write_kernel, sds((n, state), bf16))(
        inner, right_in, left_in, rows, mix_f, mix_b, read, read_r
    )

    gathered = [grad_write] + [
        lax.ppermute(grad_write, "dp", xor_pairs(dp_count, k)) for k in range(1, dp_count)
    ]
    product = lax.dot_general(
        jnp.concatenate(hidden_parts, axis=0),
        jnp.concatenate(gathered, axis=0),
        (((0,), (0,)), ((), ())),
        preferred_element_type=f32,
    )
    chips = ctx_count // 2
    piece = share // ctx_count
    product = product.reshape(chips, 2, piece, state)
    kept = lax.dynamic_index_in_dim(product, core, 1, False)
    given = lax.dynamic_index_in_dim(product, 1 - core, 1, False)
    kept = kept + lax.ppermute(given, "ctx", xor_pairs(ctx_count, 1))
    chip = ctx // 2
    total = lax.dynamic_index_in_dim(kept, chip, 0, False)
    for k in range(1, chips):
        sent = lax.dynamic_index_in_dim(kept, chip ^ k, 0, False).astype(bf16)
        total = total + lax.ppermute(sent, "ctx", xor_pairs(ctx_count, 2 * k)).astype(f32)
    grad_weight = total / (dp_count * ctx_count * n)

    write = jnp.dot(hidden, weight, preferred_element_type=f32).astype(bf16)
    grad_inner = local_call(inner_kernel, sds((n, width), bf16))(
        gf, gb, right_in, left_in, rows, cols, write, read, read_r
    )
    grad_hidden = dot_nt(grad_write, weight).astype(bf16)
    return grad_inner[None], grad_hidden[None], grad_weight


def solution(mesh):
    in_specs = (
        P("dp", "ctx", None),
        P(("dp", "ctx"), None),
        P(("dp", "ctx")),
        P("dp", "ctx", None),
        P("dp", "ctx", None),
        P("dp", None, "ctx"),
        P("dp", None, "ctx"),
        P("dp", "ctx", None),
        P("dp", "ctx", None),
    )
    out_specs = (P("dp", "ctx", None), P("dp", "ctx", None), P(("dp", "ctx"), None))
    return jax.shard_map(shards, mesh=mesh, in_specs=in_specs, out_specs=out_specs, check_vma=False)
```

```python
import functools
import itertools

import jax
import jax.numpy as jnp
from jax import lax
from jax.experimental import pallas as pl
from jax.experimental.pallas import tpu as pltpu
from jax.sharding import PartitionSpec as P

BLOCK = 128
LANES = 128
GROUP = 8
LOG2E = 1.4426950408889634
LOW = -1e30
EXACT = lax.Precision.HIGHEST
VMEM_BYTES = 14 * 1024 * 1024
BEHIND = 5 * 10**9

f32 = jnp.float32
bf16 = jnp.bfloat16

CUM2, EXCLR2, FWD_EDGE, BACK_EDGE, STEP = range(5)
C_MIX_FWD, C_MIX_BACK, C_CUM2, C_EXCL2 = range(4)


def sds(shape, dtype):
    return jax.ShapeDtypeStruct(shape, dtype)


def job(body, outs, *arrays, scalars=()):
    return body, outs, arrays, [jnp.reshape(s, (1,)).astype(jnp.int32) for s in scalars]


def run(*jobs, after=(), flops=0):
    vmem = pl.BlockSpec(memory_space=pltpu.VMEM)
    smem = pl.BlockSpec(memory_space=pltpu.SMEM)
    anywhere = pl.BlockSpec(memory_space=pl.ANY)
    ins, specs, outs, calls = [], [], [], []
    for body, job_outs, arrays, scalars in jobs:
        calls.append((body, len(ins), len(scalars) + len(arrays), len(outs), len(job_outs)))
        ins += [*scalars, *arrays]
        specs += [smem] * len(scalars) + [vmem] * len(arrays)
        outs += job_outs
    lead = len(ins) + len(after)

    def kernel(*refs):
        for body, i, ni, o, no in calls:
            body(*refs[i : i + ni], *refs[lead + o : lead + o + no])

    got = pl.pallas_call(
        kernel,
        out_shape=outs,
        in_specs=specs + [anywhere] * len(after),
        out_specs=[vmem] * len(outs),
        compiler_params=pltpu.CompilerParams(vmem_limit_bytes=VMEM_BYTES),
        cost_estimate=pl.CostEstimate(flops=flops, transcendentals=0, bytes_accessed=0),
    )(*ins, *after)
    return [list(got[o : o + no]) for _, _, _, o, no in calls]


def iotas(shape):
    return lax.broadcasted_iota(jnp.int32, shape, 0), lax.broadcasted_iota(jnp.int32, shape, 1)


def dot_nt(a, b):
    return lax.dot_general(a, b, (((1,), (1,)), ((), ())), preferred_element_type=f32)


def dot_tn(a, b):
    return lax.dot_general(a, b, (((0,), (0,)), ((), ())), preferred_element_type=f32)


def spread(rows, width):
    high = rows.astype(bf16).astype(f32)
    both = jnp.concatenate([high, rows - high], axis=0).astype(bf16)
    r, c = iotas((2 * GROUP, GROUP * width))
    pick = (r % GROUP == c // width).astype(f32).astype(bf16)
    return dot_tn(both, pick)


def tables_kernel(read_ref, decay_ref, step_ref, readr_ref, rows_ref, cols_ref):
    decay = decay_ref[...]
    heads, n = decay.shape
    r, c = iotas((n, n))
    upto = (r <= c).astype(f32)
    flip = (r + c == n - 1).astype(f32)
    readr_ref[...] = jnp.dot(
        flip.astype(bf16), read_ref[...], preferred_element_type=f32
    ).astype(bf16)
    cum = jnp.dot(decay, upto, precision=EXACT, preferred_element_type=f32)
    decay_r = jnp.dot(decay, flip, precision=EXACT, preferred_element_type=f32)
    cum_r = jnp.dot(decay_r, upto, precision=EXACT, preferred_element_type=f32)
    end = cum[:, n - 1 :]
    excl = cum - decay
    step = step_ref[...]
    log_step = jnp.log(step) * LOG2E
    cum2 = cum * LOG2E
    excl2 = excl * LOG2E
    rows_ref[CUM2] = cum2
    rows_ref[EXCLR2] = (end - cum_r) * LOG2E
    rows_ref[FWD_EDGE] = step * jnp.exp(end - cum)
    rows_ref[BACK_EDGE] = step * jnp.exp(excl)
    rows_ref[STEP] = step
    planes = (cum2 - log_step, excl2 + log_step, cum2, excl2)
    rest = jnp.zeros((LANES - GROUP * len(planes), n), f32)
    for g in range(heads // GROUP):
        part = [p[g * GROUP : (g + 1) * GROUP] for p in planes]
        cols_ref[g] = jnp.concatenate(part + [rest], axis=0).T


def part_kernel(backward, core_ref, g_ref, read_ref, decay_ref, own_ref, send_ref):
    heads, n = decay_ref.shape
    width = g_ref.shape[1] // heads
    step = GROUP * width
    r, c = iotas((n, n))
    order = ((r + c == n - 1) if backward else (r == c)).astype(f32)
    upto = (r <= c).astype(f32)
    read_t = dot_tn(read_ref[...].astype(bf16), order.astype(bf16)).astype(bf16)
    decay = decay_ref[...]
    if backward:
        decay = jnp.dot(decay, order, precision=EXACT, preferred_element_type=f32)
    weight = jnp.exp(jnp.dot(decay, upto, precision=EXACT, preferred_element_type=f32))
    state = read_t.shape[0]
    groups = heads // GROUP
    tail_row, _ = iotas((16, step))
    low = core_ref[0] == 0

    def term_of(g):
        scale = spread(weight[g * GROUP : (g + 1) * GROUP], width)
        scaled = (g_ref[:, g * step : (g + 1) * step].astype(f32) * scale).astype(bf16)
        term = jnp.dot(read_t, scaled, preferred_element_type=f32)
        last = scale[n - 1 :]
        high = last.astype(bf16).astype(f32)
        tail = jnp.where(tail_row == 0, high, jnp.where(tail_row == 1, last - high, 0.0))
        return jnp.concatenate([term, tail], axis=0)

    for g in range(groups // 2):
        here = slice(g * step, (g + 1) * step)
        lower, upper = term_of(g), term_of(g + groups // 2)
        own_ref[:, here] = jnp.where(low, lower, upper).astype(bf16)
        send_ref[:, here] = jnp.where(low, upper, lower).astype(bf16)


WIDE = 512


def chip_terms(upward, core, own_ref, near_ref):
    state = own_ref.shape[0] - 16
    first = core == (0 if upward else 1)
    for c in range(own_ref.shape[1] // WIDE):
        here = slice(c * WIDE, (c + 1) * WIDE)
        own = own_ref[:, here].astype(f32)
        other = near_ref[:, here].astype(f32)
        own_term, other_term = own[:state], other[:state]
        own_decay = own[state : state + 1] + own[state + 1 : state + 2]
        other_decay = other[state : state + 1] + other[state + 1 : state + 2]
        later = jnp.where(first, other_decay, own_decay)
        term = jnp.where(first, other_term, own_term) + later * jnp.where(
            first, own_term, other_term
        )
        yield here, term, own_decay * other_decay


def chip_kernel(upward, core_ref, own_ref, near_ref, term_ref, decay_ref):
    for here, term, decay in chip_terms(upward, core_ref[0], own_ref, near_ref):
        term_ref[:, here] = term.astype(bf16)
        decay_ref[:, here] = decay


def entered(refs, here):
    state = refs[0][:, here].astype(f32)
    for ref in refs[1:]:
        state = state + ref[:, here].astype(f32)
    return state


def onward_kernel(term_ref, decay_ref, *refs):
    *entering, out_ref = refs
    for c in range(out_ref.shape[1] // WIDE):
        here = slice(c * WIDE, (c + 1) * WIDE)
        out_ref[:, here] = (
            term_ref[:, here].astype(f32) + decay_ref[:, here] * entered(entering, here)
        ).astype(bf16)


def middle_kernel(flag_ref, term_ref, decay_ref, *refs):
    *entering, out_ref = refs
    for c in range(out_ref.shape[1] // WIDE):
        here = slice(c * WIDE, (c + 1) * WIDE)
        leaving = term_ref[:, here].astype(f32)
        if entering:
            leaving = leaving + decay_ref[:, here] * entered(entering, here)
        out_ref[:, here] = jnp.where(flag_ref[0] == 1, leaving, 0.0).astype(bf16)


def left_kernel(core_ref, own_ref, near_ref, *refs):
    *entering, out_ref = refs
    for here, term, decay in chip_terms(True, core_ref[0], own_ref, near_ref):
        out_ref[:, here] = (term + decay * entered(entering, here)).astype(bf16)


def halves_kernel(count, *refs):
    rights, lefts, out_ref = refs[:count], refs[count:-1], refs[-1]
    half = out_ref.shape[1] // 2
    for c in range(half // WIDE):
        here = slice(c * WIDE, (c + 1) * WIDE)
        there = slice(half + c * WIDE, half + (c + 1) * WIDE)
        out_ref[:, here] = entered(rights, here).astype(bf16)
        out_ref[:, there] = entered(lefts, here).astype(bf16)


def mix_kernel(fwd, inner_ref, g_ref, row_ref, cols_ref, out_ref):
    heads, n = row_ref.shape
    width = g_ref.shape[1] // heads
    step = GROUP * width
    s, t = iotas((n, n))
    keep = (t >= s) if fwd else (t + s >= n - 1)
    low_half = t < width

    def one(g, acc):
        at = pl.multiple_of(g * step, step)
        rows = row_ref[pl.ds(pl.multiple_of(g * GROUP, GROUP), GROUP)]
        cols = cols_ref[g]
        for pair in range(GROUP // 2):
            here = pl.ds(at + pair * LANES, LANES)
            inner = inner_ref[:, here].astype(f32)
            halves = jnp.concatenate(
                [jnp.where(low_half, inner, 0.0), jnp.where(low_half, 0.0, inner)], axis=0
            ).astype(bf16)
            dots = dot_nt(halves, g_ref[:, here])
            for j in range(2):
                h = 2 * pair + j
                row = rows[h : h + 1]
                if fwd:
                    k = C_MIX_FWD * GROUP + h
                    power = row - cols[:, k : k + 1]
                else:
                    k = C_MIX_BACK * GROUP + h
                    power = cols[:, k : k + 1] - row
                decay = jnp.exp2(jnp.where(keep, power, LOW))
                acc = acc + decay * dots[j * n : (j + 1) * n]
        return acc

    out_ref[...] = lax.fori_loop(0, heads // GROUP, one, jnp.zeros((n, n), f32))


def edge_terms(
    upward, core, inner_ref, halves_ref, swapped_ref, near_ref, far_ref, edge, state_ref
):
    heads, n = edge.shape
    width = inner_ref.shape[1] // heads
    step = GROUP * width
    groups = heads // GROUP
    first = core == (0 if upward else 1)
    rows = state_ref.shape[0]
    base = halves_ref.shape[1] // 2 if upward else 0
    acc = 0.0
    for g in range(groups):
        here = slice(g * step, (g + 1) * step)
        at = base + g % (groups // 2) * step
        there = slice(at, at + step)
        near = slice(at - base, at - base + step)
        mine = core == g // (groups // 2)
        whole = jnp.where(mine, halves_ref[:, there].astype(f32), swapped_ref[:, there].astype(f32))
        other = jnp.where(mine, near_ref[:, near].astype(f32), far_ref[:, near].astype(f32))
        decay = other[rows : rows + 1] + other[rows + 1 : rows + 2]
        entering = jnp.where(first, whole, other[:rows] + decay * whole).astype(bf16)
        state_ref[:, here] = entering
        scaled = inner_ref[:, here].astype(f32) * spread(edge[g * GROUP : (g + 1) * GROUP], width)
        acc = acc + dot_nt(scaled.astype(bf16), entering)
    return acc


def write_kernel(
    core_ref,
    inner_ref,
    halves_ref,
    swapped_ref,
    right_near_ref,
    right_far_ref,
    left_near_ref,
    left_far_ref,
    rows_ref,
    mixf_ref,
    mixb_ref,
    read_ref,
    readr_ref,
    right_ref,
    left_ref,
    out_ref,
):
    core = core_ref[0]
    shared = (inner_ref, halves_ref, swapped_ref)
    acc = jnp.dot(mixf_ref[...].astype(bf16), read_ref[...], preferred_element_type=f32)
    acc = acc + jnp.dot(mixb_ref[...].astype(bf16), readr_ref[...], preferred_element_type=f32)
    acc = acc + edge_terms(False, core, *shared, right_near_ref, right_far_ref, rows_ref[FWD_EDGE], right_ref)
    acc = acc + edge_terms(True, core, *shared, left_near_ref, left_far_ref, rows_ref[BACK_EDGE], left_ref)
    out_ref[...] = acc.astype(bf16)


def share_kernel(dp_ref, hidden_ref, weight_ref, *out_refs):
    share = weight_ref.shape[0]
    for k, out_ref in enumerate(out_refs):
        for c in range(share // LANES):
            at = pl.multiple_of((dp_ref[0] ^ k) * share + c * LANES, LANES)
            out_ref[c * LANES : (c + 1) * LANES] = (
                hidden_ref[:, pl.ds(at, LANES)].astype(f32).T.astype(bf16)
            )
        out_ref[share:] = weight_ref[...]


def product_kernel(core_ref, *refs):
    count = (len(refs) - 2) // 2
    hidden_refs, write_refs = refs[:count], refs[count : 2 * count]
    keep_ref, give_ref = refs[2 * count :]
    chips, piece, _ = keep_ref.shape
    writes = [w[...] for w in write_refs]
    for which, out_ref in ((core_ref[0], keep_ref), (1 - core_ref[0], give_ref)):
        for chip in range(chips):
            rows = pl.ds(pl.multiple_of((2 * chip + which) * piece, piece), piece)
            total = jnp.dot(hidden_refs[0][rows], writes[0], preferred_element_type=f32)
            for k in range(1, count):
                total = total + jnp.dot(hidden_refs[k][rows], writes[k], preferred_element_type=f32)
            out_ref[chip] = total.astype(out_ref.dtype)


def deal_kernel(chip_ref, keep_ref, got_ref, own_ref, *out_refs):
    chip = chip_ref[0]
    own_ref[...] = keep_ref[chip] + got_ref[chip].astype(f32)
    for k, out_ref in enumerate(out_refs, 1):
        out_ref[...] = (keep_ref[chip ^ k] + got_ref[chip ^ k].astype(f32)).astype(bf16)


def cut_kernel(start, array_ref, out_ref):
    out_ref[...] = array_ref[:, start : start + out_ref.shape[1]]


def stack_kernel(*refs):
    *arrays, out_ref = refs
    for k, ref in enumerate(arrays):
        out_ref[k] = ref[...].astype(bf16)


def pair_kernel(chip_ref, core_ref, held_ref, got_ref, out_ref):
    chip, core = chip_ref[0], core_ref[0]
    chips = held_ref.shape[0]
    for k in range(chips):
        held_core = core if k < chips - 1 else 1 - core
        out_ref[chip ^ k, held_core] = held_ref[k]
        out_ref[chip ^ k, 1 - held_core] = got_ref[k]


def gather_kernel(index_ref, *refs):
    *arrays, out_ref = refs
    rows = out_ref.shape[1]
    for k, ref in enumerate(arrays):
        out_ref[index_ref[0] ^ k] = ref[ref.shape[0] - rows :]


def inner_kernel(
    gf_ref, gb_ref, right_ref, left_ref, rows_ref, cols_ref, write_ref, read_ref, readr_ref, out_ref
):
    _, heads, n = rows_ref.shape
    width = gf_ref.shape[1] // heads
    step = GROUP * width
    write = write_ref[...]
    kernel_f = dot_nt(write, read_ref[...])
    kernel_b = dot_nt(write, readr_ref[...])
    s, t = iotas((n, n))
    low_half = t < width

    def one(g, carry):
        at = pl.multiple_of(g * step, step)
        own = pl.ds(pl.multiple_of(g * GROUP, GROUP), GROUP)
        cols = cols_ref[g]
        cum2 = rows_ref[CUM2, own]
        exclr2 = rows_ref[EXCLR2, own]
        step_e = spread(rows_ref[STEP, own], width)
        edges = spread(rows_ref[FWD_EDGE, own], width) * jnp.dot(
            write, right_ref[:, pl.ds(at, step)], preferred_element_type=f32
        )
        edges = edges + spread(rows_ref[BACK_EDGE, own], width) * jnp.dot(
            write, left_ref[:, pl.ds(at, step)], preferred_element_type=f32
        )
        for pair in range(GROUP // 2):
            mixes = []
            for j in range(2):
                h = 2 * pair + j
                kf = C_CUM2 * GROUP + h
                kb = C_EXCL2 * GROUP + h
                pf = cum2[h : h + 1] - cols[:, kf : kf + 1]
                pb = cols[:, kb : kb + 1] - exclr2[h : h + 1]
                mf = jnp.exp2(jnp.where(t >= s, pf, LOW)) * kernel_f
                mb = jnp.exp2(jnp.where(t + s >= n - 1, pb, LOW)) * kernel_b
                mixes.append(jnp.concatenate([mf, mb], axis=1))
            here = pl.ds(at + pair * LANES, LANES)
            both = jnp.concatenate([gf_ref[:, here], gb_ref[:, here]], axis=0)
            got = jnp.dot(
                jnp.concatenate(mixes, axis=0).astype(bf16), both, preferred_element_type=f32
            )
            intra = jnp.where(low_half, got[:n], got[n:])
            mine = slice(pair * LANES, (pair + 1) * LANES)
            out_ref[:, here] = (step_e[:, mine] * intra + edges[:, mine]).astype(bf16)
        return carry

    lax.fori_loop(0, heads // GROUP, one, 0)


def xor_pairs(count, k):
    return [(i, i ^ k) for i in range(count)]


def chip_pairs(moves):
    return [(2 * a + i, 2 * b + i) for a, b in moves for i in range(2)]


def shards(
    hidden_in,
    write_weight,
    shard_scale,
    inner_acts,
    read_proj,
    step_size,
    log_decay,
    grad_fwd,
    grad_rev,
):
    ctx_count = lax.axis_size("ctx")
    dp_count = lax.axis_size("dp")
    ctx = lax.axis_index("ctx")
    dp = lax.axis_index("dp")
    core, chip = ctx % 2, ctx // 2
    chips = ctx_count // 2
    span = chips // 2
    hidden = hidden_in[0]
    inner = inner_acts[0]
    read = read_proj[0]
    step = step_size[0]
    decay = log_decay[0]
    gf = grad_fwd[0]
    gr = grad_rev[0]
    n, width = inner.shape
    heads = decay.shape[0]
    state = read.shape[1]
    half = width // 2
    share = hidden.shape[1] // dp_count
    part = functools.partial
    part_shapes = [sds((state + 16, half), bf16)] * 2
    half_shape = sds((state, half), bf16)
    chip_shapes = [half_shape, sds((1, half), f32)]

    def over_cores(array):
        return lax.ppermute(array, "ctx", xor_pairs(ctx_count, 1))

    def over_chips(array, *moves):
        return lax.ppermute(array, "ctx", chip_pairs(moves))

    def over_dp(array, k):
        return lax.ppermute(array, "dp", xor_pairs(dp_count, k))

    def flip(piece):
        return lax.ppermute(piece, "ctx", [(i, ctx_count - 1 - i) for i in range(ctx_count)])

    local = (write_weight.astype(f32) * shard_scale[0]).astype(bf16)
    mirrored = flip(jnp.concatenate([read.astype(f32), decay, local.astype(f32)], axis=0))
    weights = [local] + [
        lax.ppermute(local, "ctx", xor_pairs(ctx_count, 2 * k)) for k in range(1, chips - 1)
    ]
    gr_again, *_ = lax.optimization_barrier((gr, mirrored, *weights))
    flipped = flip(gr_again)

    def part_job(backward, *arrays):
        return job(part(part_kernel, backward), part_shapes, *arrays, scalars=(core,))

    def chip_job(upward, own, near):
        return job(part(chip_kernel, upward), chip_shapes, own, near, scalars=(core,))

    (early_own, send), (held,) = run(
        part_job(True, gr, mirrored[:n], mirrored[n : n + heads]),
        job(stack_kernel, [sds((chips, *local.shape), bf16)], *weights, mirrored[n + heads :]),
    )
    early_near = over_cores(send)
    ((right_own, send),) = run(part_job(False, gf, read, decay))
    right_near = over_cores(send)
    (early_term, early_decay), (read_r, rows, cols) = run(
        chip_job(False, early_own, early_near),
        job(
            tables_kernel,
            [
                sds((n, state), bf16),
                sds((5, heads, n), f32),
                sds((heads // GROUP, n, LANES), f32),
            ],
            read,
            decay,
            step,
        ),
        after=(right_own,),
    )
    earlies = []
    for i in range(span - 1):
        leaving = early_term
        if i:
            ((leaving,),) = run(
                job(onward_kernel, [half_shape], early_term, early_decay, *earlies)
            )
        earlies.append(over_chips(leaving, (chips - 1 - i, chips - 2 - i)))
    ((right_term, right_decay),) = run(
        chip_job(False, right_own, right_near), after=(early_term,)
    )
    rights = [over_chips(right_term, (chips - 1, chips - 2))]
    got = over_cores(held)
    ((held,),) = run(
        job(
            pair_kernel,
            [sds((chips, 2, *local.shape), bf16)],
            held,
            got,
            scalars=(chip, core),
        ),
        after=(right_term,),
    )
    held = held.reshape(-1, state)
    (shares,) = run(
        job(share_kernel, [sds((2 * share, n), bf16)] * dp_count, hidden, held, scalars=(dp,))
    )
    shared = [shares[0]] + [over_dp(shares[k], k) for k in range(1, dp_count)]
    ((mix_f,),) = run(
        job(part(mix_kernel, True), [sds((n, n), f32)], inner, gf, rows[CUM2], cols),
        after=(right_term,),
    )
    right_far = over_cores(right_own)
    ((leaving,),) = run(
        job(onward_kernel, [half_shape], right_term, right_decay, *rights),
        after=(mix_f, right_far, *earlies, *shared[1:3]),
    )
    rights.append(over_chips(leaving, (chips - 2, chips - 3)))

    ((left_own, send),) = run(part_job(True, flipped, read, decay), after=(leaving,))
    left_near = over_cores(send)
    ((middle,),) = run(
        job(
            middle_kernel, [half_shape], early_term, early_decay, *earlies, scalars=(chip == span,)
        ),
        after=(left_own,),
    )
    lefts = [middle]
    for i in range(span - 1):
        ((leaving,),) = run(
            job(left_kernel, [half_shape], left_own, left_near, *lefts, scalars=(core,))
        )
        lefts.append(over_chips(leaving, (i, i + 1), (span + i, span + i + 1)))
    ((mix_b,),) = run(
        job(part(mix_kernel, False), [sds((n, n), f32)], inner, flipped, rows[EXCLR2], cols),
        after=(leaving,),
    )
    left_far = over_cores(left_own)
    for i in range(2, chips - 1):
        ((leaving,),) = run(
            job(onward_kernel, [half_shape], right_term, right_decay, *rights),
            after=(mix_b, *shared[3:]) if i == 2 else (),
            flops=BEHIND,
        )
        rights.append(over_chips(leaving, (chips - 1 - i, chips - 2 - i)))
    ((halves,),) = run(
        job(part(halves_kernel, len(rights)), [sds((state, width), bf16)], *rights, *lefts),
        after=(left_far,),
    )
    swapped = over_cores(halves)

    ((right_in, left_in, grad_write),) = run(
        job(
            write_kernel,
            [sds((state, width), bf16), sds((state, width), bf16), sds((n, state), bf16)],
            inner,
            halves,
            swapped,
            right_near,
            right_far,
            left_near,
            left_far,
            rows,
            mix_f,
            mix_b,
            read,
            read_r,
            scalars=(core,),
        )
    )
    gb = flipped

    writes = [grad_write] + [over_dp(grad_write, k) for k in range(1, dp_count)]
    ((weight,),) = run(
        job(gather_kernel, [sds((dp_count, share, state), bf16)], *shared, scalars=(dp,)),
        after=(grad_write,),
    )
    weight = weight.reshape(-1, state)
    write = jnp.dot(hidden, weight, preferred_element_type=f32).astype(bf16)
    ((grad_inner,),) = run(
        job(
            inner_kernel,
            [sds((n, width), bf16)],
            gf,
            gb,
            right_in,
            left_in,
            rows,
            cols,
            write,
            read,
            read_r,
        )
    )
    piece = share // ctx_count
    ((keep, give),) = run(
        job(
            product_kernel,
            [sds((chips, piece, state), f32), sds((chips, piece, state), bf16)],
            *shared,
            *writes,
            scalars=(core,),
        ),
        after=(grad_inner,),
    )
    ((total, *dealt),) = run(
        job(
            deal_kernel,
            [sds((piece, state), f32)] + [sds((piece, state), bf16)] * (chips - 1),
            keep,
            over_cores(give),
            scalars=(chip,),
        )
    )
    for k in range(1, chips):
        total = total + lax.ppermute(dealt[k - 1], "ctx", xor_pairs(ctx_count, 2 * k)).astype(f32)
    grad_weight = total / (dp_count * ctx_count * n)

    grad_hidden = dot_nt(grad_write, weight).astype(bf16)
    return grad_inner[None], grad_hidden[None], grad_weight


def solution(mesh):
    in_specs = (
        P("dp", "ctx", None),
        P(("dp", "ctx"), None),
        P(("dp", "ctx")),
        P("dp", "ctx", None),
        P("dp", "ctx", None),
        P("dp", None, "ctx"),
        P("dp", None, "ctx"),
        P("dp", "ctx", None),
        P("dp", "ctx", None),
    )
    out_specs = (P("dp", "ctx", None), P("dp", "ctx", None), P(("dp", "ctx"), None))
    return jax.shard_map(shards, mesh=mesh, in_specs=in_specs, out_specs=out_specs, check_vma=False)
```

```python
import functools
import itertools

import jax
import jax.numpy as jnp
from jax import lax
from jax.experimental import pallas as pl
from jax.experimental.pallas import tpu as pltpu
from jax.sharding import PartitionSpec as P

BLOCK = 128
LANES = 128
GROUP = 8
LOG2E = 1.4426950408889634
LOW = -1e30
EXACT = lax.Precision.HIGHEST
VMEM_BYTES = 14 * 1024 * 1024
CUT = 1024
PIECES = 2

f32 = jnp.float32
bf16 = jnp.bfloat16

CUM2, EXCLR2, FWD_EDGE, BACK_EDGE, STEP = range(5)
C_MIX_FWD, C_MIX_BACK, C_CUM2, C_EXCL2 = range(4)


def sds(shape, dtype):
    return jax.ShapeDtypeStruct(shape, dtype)


def job(body, outs, *arrays, scalars=()):
    return body, outs, arrays, [jnp.reshape(s, (1,)).astype(jnp.int32) for s in scalars]


def run(*jobs, after=(), flops=0):
    vmem = pl.BlockSpec(memory_space=pltpu.VMEM)
    smem = pl.BlockSpec(memory_space=pltpu.SMEM)
    anywhere = pl.BlockSpec(memory_space=pl.ANY)
    ins, specs, outs, calls = [], [], [], []
    for body, job_outs, arrays, scalars in jobs:
        calls.append((body, len(ins), len(scalars) + len(arrays), len(outs), len(job_outs)))
        ins += [*scalars, *arrays]
        specs += [smem] * len(scalars) + [vmem] * len(arrays)
        outs += job_outs
    lead = len(ins) + len(after)

    def kernel(*refs):
        for body, i, ni, o, no in calls:
            body(*refs[i : i + ni], *refs[lead + o : lead + o + no])

    got = pl.pallas_call(
        kernel,
        out_shape=outs,
        in_specs=specs + [anywhere] * len(after),
        out_specs=[vmem] * len(outs),
        compiler_params=pltpu.CompilerParams(vmem_limit_bytes=VMEM_BYTES),
        cost_estimate=pl.CostEstimate(flops=flops, transcendentals=0, bytes_accessed=flops // 250),
    )(*ins, *after)
    return [list(got[o : o + no]) for _, _, _, o, no in calls]


def run_on_half(body, side, shape, arrays, before, after=()):
    vmem = pl.BlockSpec(memory_space=pltpu.VMEM)
    anywhere = pl.BlockSpec(memory_space=pl.ANY)
    rest = [*before, *after]

    def kernel(*refs):
        body(*refs[: len(arrays)], refs[-1])

    return pl.pallas_call(
        kernel,
        grid=(1,),
        out_shape=shape,
        in_specs=[vmem] * len(arrays) + [anywhere] * len(rest),
        out_specs=pl.BlockSpec((shape.shape[0], shape.shape[1] // 2), lambda i: (0, side)),
        input_output_aliases={len(arrays): 0} if before else {},
        compiler_params=pltpu.CompilerParams(vmem_limit_bytes=VMEM_BYTES),
        cost_estimate=pl.CostEstimate(flops=0, transcendentals=0, bytes_accessed=0),
    )(*arrays, *rest)


def iotas(shape):
    return lax.broadcasted_iota(jnp.int32, shape, 0), lax.broadcasted_iota(jnp.int32, shape, 1)


def dot_nt(a, b):
    return lax.dot_general(a, b, (((1,), (1,)), ((), ())), preferred_element_type=f32)


def dot_tn(a, b):
    return lax.dot_general(a, b, (((0,), (0,)), ((), ())), preferred_element_type=f32)


def spread(rows, width):
    high = rows.astype(bf16).astype(f32)
    both = jnp.concatenate([high, rows - high], axis=0).astype(bf16)
    r, c = iotas((2 * GROUP, GROUP * width))
    pick = (r % GROUP == c // width).astype(f32).astype(bf16)
    return dot_tn(both, pick)


def tables_kernel(read_ref, decay_ref, step_ref, readr_ref, rows_ref, cols_ref):
    decay = decay_ref[...]
    heads, n = decay.shape
    r, c = iotas((n, n))
    upto = (r <= c).astype(f32)
    flip = (r + c == n - 1).astype(f32)
    readr_ref[...] = jnp.dot(
        flip.astype(bf16), read_ref[...], preferred_element_type=f32
    ).astype(bf16)
    cum = jnp.dot(decay, upto, precision=EXACT, preferred_element_type=f32)
    decay_r = jnp.dot(decay, flip, precision=EXACT, preferred_element_type=f32)
    cum_r = jnp.dot(decay_r, upto, precision=EXACT, preferred_element_type=f32)
    end = cum[:, n - 1 :]
    excl = cum - decay
    step = step_ref[...]
    log_step = jnp.log(step) * LOG2E
    cum2 = cum * LOG2E
    excl2 = excl * LOG2E
    rows_ref[CUM2] = cum2
    rows_ref[EXCLR2] = (end - cum_r) * LOG2E
    rows_ref[FWD_EDGE] = step * jnp.exp(end - cum)
    rows_ref[BACK_EDGE] = step * jnp.exp(excl)
    rows_ref[STEP] = step
    planes = (cum2 - log_step, excl2 + log_step, cum2, excl2)
    rest = jnp.zeros((LANES - GROUP * len(planes), n), f32)
    for g in range(heads // GROUP):
        part = [p[g * GROUP : (g + 1) * GROUP] for p in planes]
        cols_ref[g] = jnp.concatenate(part + [rest], axis=0).T


def columns(refs, at, count, value=None):
    for ref in refs:
        if at < ref.shape[1]:
            if value is None:
                return ref[:, at : at + count]
            ref[:, at : at + count] = value
            return None
        at -= ref.shape[1]


def part_kernel(backward, count, core_ref, *refs):
    g_refs, (read_ref, decay_ref, own_ref, *send_refs) = refs[:count], refs[count:]
    heads, n = decay_ref.shape
    width = sum(ref.shape[1] for ref in g_refs) // heads
    step = GROUP * width
    r, c = iotas((n, n))
    order = ((r + c == n - 1) if backward else (r == c)).astype(f32)
    upto = (r <= c).astype(f32)
    read_t = dot_tn(read_ref[...].astype(bf16), order.astype(bf16)).astype(bf16)
    decay = decay_ref[...]
    if backward:
        decay = jnp.dot(decay, order, precision=EXACT, preferred_element_type=f32)
    weight = jnp.exp(jnp.dot(decay, upto, precision=EXACT, preferred_element_type=f32))
    state = read_t.shape[0]
    groups = heads // GROUP
    tail_row, _ = iotas((16, step))
    low = core_ref[0] == 0

    def term_of(g):
        scale = spread(weight[g * GROUP : (g + 1) * GROUP], width)
        cotangent = columns(g_refs, g * step, step)
        scaled = (cotangent.astype(f32) * scale).astype(bf16)
        term = jnp.dot(read_t, scaled, preferred_element_type=f32)
        last = scale[n - 1 :]
        high = last.astype(bf16).astype(f32)
        tail = jnp.where(tail_row == 0, high, jnp.where(tail_row == 1, last - high, 0.0))
        return jnp.concatenate([term, tail], axis=0)

    for g in range(groups // 2):
        here = slice(g * step, (g + 1) * step)
        lower, upper = term_of(g), term_of(g + groups // 2)
        own_ref[:, here] = jnp.where(low, lower, upper).astype(bf16)
        sent = jnp.where(low, upper, lower).astype(bf16)
        columns(send_refs, g * step, step, sent)


WIDE = 512


def chip_terms(upward, core, own_ref, near_refs):
    state = own_ref.shape[0] - 16
    first = core == (0 if upward else 1)
    for c in range(own_ref.shape[1] // WIDE):
        here = slice(c * WIDE, (c + 1) * WIDE)
        own = own_ref[:, here].astype(f32)
        other = columns(near_refs, c * WIDE, WIDE).astype(f32)
        own_term, other_term = own[:state], other[:state]
        own_decay = own[state : state + 1] + own[state + 1 : state + 2]
        other_decay = other[state : state + 1] + other[state + 1 : state + 2]
        later = jnp.where(first, other_decay, own_decay)
        term = jnp.where(first, other_term, own_term) + later * jnp.where(
            first, own_term, other_term
        )
        yield here, term, own_decay * other_decay


def chip_kernel(upward, core_ref, own_ref, *refs):
    *near_refs, term_ref, decay_ref = refs
    for here, term, decay in chip_terms(upward, core_ref[0], own_ref, near_refs):
        term_ref[:, here] = term.astype(bf16)
        decay_ref[:, here] = decay


def entered(refs, here):
    state = refs[0][:, here].astype(f32)
    for ref in refs[1:]:
        state = state + ref[:, here].astype(f32)
    return state


def onward_kernel(term_ref, decay_ref, *refs):
    *entering, out_ref = refs
    for c in range(out_ref.shape[1] // WIDE):
        here = slice(c * WIDE, (c + 1) * WIDE)
        out_ref[:, here] = (
            term_ref[:, here].astype(f32) + decay_ref[:, here] * entered(entering, here)
        ).astype(bf16)


def middle_kernel(flag_ref, term_ref, decay_ref, *refs):
    *entering, out_ref = refs
    for c in range(out_ref.shape[1] // WIDE):
        here = slice(c * WIDE, (c + 1) * WIDE)
        leaving = term_ref[:, here].astype(f32)
        if entering:
            leaving = leaving + decay_ref[:, here] * entered(entering, here)
        out_ref[:, here] = jnp.where(flag_ref[0] == 1, leaving, 0.0).astype(bf16)


def left_kernel(count, core_ref, flag_ref, own_ref, *refs):
    near_refs, early, refs = refs[:PIECES], refs[PIECES : PIECES + count], refs[PIECES + count :]
    if early:
        out_ref, middle_ref = refs
        middle_kernel(flag_ref, *early, middle_ref)
        entering = [middle_ref]
    else:
        *entering, out_ref = refs
    for here, term, decay in chip_terms(True, core_ref[0], own_ref, near_refs):
        out_ref[:, here] = (term + decay * entered(entering, here)).astype(bf16)


def halves_kernel(count, *refs):
    rights, lefts, out_ref = refs[:count], refs[count:-1], refs[-1]
    half = out_ref.shape[1] // 2
    for c in range(half // WIDE):
        here = slice(c * WIDE, (c + 1) * WIDE)
        there = slice(half + c * WIDE, half + (c + 1) * WIDE)
        out_ref[:, here] = entered(rights, here).astype(bf16)
        out_ref[:, there] = entered(lefts, here).astype(bf16)


def mix_kernel(fwd, count, *refs):
    g_refs, (inner_ref, row_ref, cols_ref, out_ref) = refs[:count], refs[count:]
    heads, n = row_ref.shape
    width = inner_ref.shape[1] // heads
    step = GROUP * width
    s, t = iotas((n, n))
    keep = (t >= s) if fwd else (t + s >= n - 1)
    low_half = t < width
    acc = jnp.zeros((n, n), f32)
    first = 0
    for g_ref in g_refs:
        groups = g_ref.shape[1] // step

        def one(g, acc, g_ref=g_ref, first=first):
            at = pl.multiple_of(g * step, step)
            base = pl.multiple_of((first + g) * step, step)
            rows = row_ref[pl.ds(pl.multiple_of((first + g) * GROUP, GROUP), GROUP)]
            cols = cols_ref[first + g]
            for pair in range(GROUP // 2):
                inner = inner_ref[:, pl.ds(base + pair * LANES, LANES)].astype(f32)
                halves = jnp.concatenate(
                    [jnp.where(low_half, inner, 0.0), jnp.where(low_half, 0.0, inner)], axis=0
                ).astype(bf16)
                dots = dot_nt(halves, g_ref[:, pl.ds(at + pair * LANES, LANES)])
                for j in range(2):
                    h = 2 * pair + j
                    row = rows[h : h + 1]
                    if fwd:
                        k = C_MIX_FWD * GROUP + h
                        power = row - cols[:, k : k + 1]
                    else:
                        k = C_MIX_BACK * GROUP + h
                        power = cols[:, k : k + 1] - row
                    decay = jnp.exp2(jnp.where(keep, power, LOW))
                    acc = acc + decay * dots[j * n : (j + 1) * n]
            return acc

        acc = lax.fori_loop(0, groups, one, acc)
        first += groups
    out_ref[...] = acc


def edge_terms(
    upward, core, inner_ref, halves_ref, swapped_ref, near_refs, far_ref, edge, state_ref
):
    heads, n = edge.shape
    width = inner_ref.shape[1] // heads
    step = GROUP * width
    groups = heads // GROUP
    first = core == (0 if upward else 1)
    rows = state_ref.shape[0]
    base = halves_ref.shape[1] // 2 if upward else 0
    acc = 0.0
    for g in range(groups):
        here = slice(g * step, (g + 1) * step)
        at = base + g % (groups // 2) * step
        there = slice(at, at + step)
        near = slice(at - base, at - base + step)
        mine = core == g // (groups // 2)
        whole = jnp.where(mine, halves_ref[:, there].astype(f32), swapped_ref[:, there].astype(f32))
        other = columns(near_refs, at - base, step).astype(f32)
        other = jnp.where(mine, other, far_ref[:, near].astype(f32))
        decay = other[rows : rows + 1] + other[rows + 1 : rows + 2]
        entering = jnp.where(first, whole, other[:rows] + decay * whole).astype(bf16)
        state_ref[:, here] = entering
        scaled = inner_ref[:, here].astype(f32) * spread(edge[g * GROUP : (g + 1) * GROUP], width)
        acc = acc + dot_nt(scaled.astype(bf16), entering)
    return acc


def write_kernel(
    core_ref,
    inner_ref,
    halves_ref,
    swapped_ref,
    right_far_ref,
    left_far_ref,
    rows_ref,
    mixf_ref,
    mixb_ref,
    read_ref,
    readr_ref,
    *refs,
):
    right_near_refs, left_near_refs = refs[:PIECES], refs[PIECES : 2 * PIECES]
    right_ref, left_ref, out_ref = refs[2 * PIECES :]
    core = core_ref[0]
    shared = (inner_ref, halves_ref, swapped_ref)
    acc = jnp.dot(mixf_ref[...].astype(bf16), read_ref[...], preferred_element_type=f32)
    acc = acc + jnp.dot(mixb_ref[...].astype(bf16), readr_ref[...], preferred_element_type=f32)
    right_edge, left_edge = rows_ref[FWD_EDGE], rows_ref[BACK_EDGE]
    acc = acc + edge_terms(
        False, core, *shared, right_near_refs, right_far_ref, right_edge, right_ref
    )
    acc = acc + edge_terms(True, core, *shared, left_near_refs, left_far_ref, left_edge, left_ref)
    out_ref[...] = acc.astype(bf16)


def share_kernel(dp_ref, hidden_ref, weight_ref, *out_refs):
    share = weight_ref.shape[0]
    for k, out_ref in enumerate(out_refs):
        for c in range(share // LANES):
            at = pl.multiple_of((dp_ref[0] ^ k) * share + c * LANES, LANES)
            out_ref[c * LANES : (c + 1) * LANES] = (
                hidden_ref[:, pl.ds(at, LANES)].astype(f32).T.astype(bf16)
            )
        out_ref[share:] = weight_ref[...]


def product_kernel(core_ref, *refs):
    count = (len(refs) - 2) // 2
    hidden_refs, write_refs = refs[:count], refs[count : 2 * count]
    keep_ref, give_ref = refs[2 * count :]
    chips, piece, _ = keep_ref.shape
    writes = [w[...] for w in write_refs]
    for which, out_ref in ((core_ref[0], keep_ref), (1 - core_ref[0], give_ref)):
        for chip in range(chips):
            rows = pl.ds(pl.multiple_of((2 * chip + which) * piece, piece), piece)
            total = jnp.dot(hidden_refs[0][rows], writes[0], preferred_element_type=f32)
            for k in range(1, count):
                total = total + jnp.dot(hidden_refs[k][rows], writes[k], preferred_element_type=f32)
            out_ref[chip] = total.astype(out_ref.dtype)


def deal_kernel(chip_ref, keep_ref, got_ref, own_ref, *out_refs):
    chip = chip_ref[0]
    own_ref[...] = keep_ref[chip] + got_ref[chip].astype(f32)
    for k, out_ref in enumerate(out_refs, 1):
        out_ref[...] = (keep_ref[chip ^ k] + got_ref[chip ^ k].astype(f32)).astype(bf16)


def cut_kernel(start, array_ref, out_ref):
    out_ref[...] = array_ref[:, start : start + out_ref.shape[1]]


def stack_kernel(*refs):
    *arrays, out_ref = refs
    for k, ref in enumerate(arrays):
        out_ref[k] = ref[...].astype(bf16)


def pair_kernel(chip_ref, core_ref, held_ref, got_ref, out_ref):
    chip, core = chip_ref[0], core_ref[0]
    chips = held_ref.shape[0]
    for k in range(chips):
        held_core = core if k < chips - 1 else 1 - core
        out_ref[chip ^ k, held_core] = held_ref[k]
        out_ref[chip ^ k, 1 - held_core] = got_ref[k]


def gather_kernel(index_ref, *refs):
    *arrays, out_ref = refs
    rows = out_ref.shape[1]
    for k, ref in enumerate(arrays):
        out_ref[index_ref[0] ^ k] = ref[ref.shape[0] - rows :]


def inner_kernel(
    side, gf_ref, right_ref, left_ref, rows_ref, cols_ref, write_ref, read_ref, readr_ref, *refs
):
    *gb_refs, out_ref = refs
    _, heads, n = rows_ref.shape
    width = gf_ref.shape[1] // heads
    step = GROUP * width
    half = heads // GROUP // 2
    write = write_ref[...]
    kernel_f = dot_nt(write, read_ref[...])
    kernel_b = dot_nt(write, readr_ref[...])
    s, t = iotas((n, n))
    low_half = t < width

    for g in range(side * half, (side + 1) * half):
        at = g * step
        own = slice(g * GROUP, (g + 1) * GROUP)
        whole = slice(at, at + step)
        cols = cols_ref[g]
        cum2 = rows_ref[CUM2, own]
        exclr2 = rows_ref[EXCLR2, own]
        step_e = spread(rows_ref[STEP, own], width)
        edges = spread(rows_ref[FWD_EDGE, own], width) * jnp.dot(
            write, right_ref[:, whole], preferred_element_type=f32
        )
        edges = edges + spread(rows_ref[BACK_EDGE, own], width) * jnp.dot(
            write, left_ref[:, whole], preferred_element_type=f32
        )
        for pair in range(GROUP // 2):
            mixes = []
            for j in range(2):
                h = 2 * pair + j
                kf = C_CUM2 * GROUP + h
                kb = C_EXCL2 * GROUP + h
                pf = cum2[h : h + 1] - cols[:, kf : kf + 1]
                pb = cols[:, kb : kb + 1] - exclr2[h : h + 1]
                mf = jnp.exp2(jnp.where(t >= s, pf, LOW)) * kernel_f
                mb = jnp.exp2(jnp.where(t + s >= n - 1, pb, LOW)) * kernel_b
                mixes.append(jnp.concatenate([mf, mb], axis=1))
            here = at + pair * LANES
            both = jnp.concatenate(
                [gf_ref[:, here : here + LANES], columns(gb_refs, here, LANES)], axis=0
            )
            got = jnp.dot(
                jnp.concatenate(mixes, axis=0).astype(bf16), both, preferred_element_type=f32
            )
            intra = jnp.where(low_half, got[:n], got[n:])
            mine = slice(pair * LANES, (pair + 1) * LANES)
            into = (g - side * half) * step + pair * LANES
            out_ref[:, into : into + LANES] = (step_e[:, mine] * intra + edges[:, mine]).astype(
                bf16
            )


def xor_pairs(count, k):
    return [(i, i ^ k) for i in range(count)]


def chip_pairs(moves):
    return [(2 * a + i, 2 * b + i) for a, b in moves for i in range(2)]


def shards(
    hidden_in,
    write_weight,
    shard_scale,
    inner_acts,
    read_proj,
    step_size,
    log_decay,
    grad_fwd,
    grad_rev,
):
    ctx_count = lax.axis_size("ctx")
    dp_count = lax.axis_size("dp")
    ctx = lax.axis_index("ctx")
    dp = lax.axis_index("dp")
    core, chip = ctx % 2, ctx // 2
    chips = ctx_count // 2
    span = chips // 2
    hidden = hidden_in[0]
    inner = inner_acts[0]
    read = read_proj[0]
    step = step_size[0]
    decay = log_decay[0]
    gf = grad_fwd[0]
    gr = grad_rev[0]
    n, width = inner.shape
    heads = decay.shape[0]
    state = read.shape[1]
    half = width // 2
    share = hidden.shape[1] // dp_count
    part = functools.partial
    part_shapes = [sds((state + 16, half), bf16)]
    part_shapes += [sds((state + 16, half // PIECES), bf16)] * PIECES
    half_shape = sds((state, half), bf16)
    chip_shapes = [half_shape, sds((1, half), f32)]

    def over_cores(array):
        return lax.ppermute(array, "ctx", xor_pairs(ctx_count, 1))

    def over_chips(array, *moves):
        return lax.ppermute(array, "ctx", chip_pairs(moves))

    def over_dp(array, k):
        return lax.ppermute(array, "dp", xor_pairs(dp_count, k))

    def flip(piece):
        return lax.ppermute(piece, "ctx", [(i, ctx_count - 1 - i) for i in range(ctx_count)])

    local = (write_weight.astype(f32) * shard_scale[0]).astype(bf16)
    mirrored = flip(jnp.concatenate([read.astype(f32), decay, local.astype(f32)], axis=0))
    weights = [local] + [
        lax.ppermute(local, "ctx", xor_pairs(ctx_count, 2 * k)) for k in range(1, chips - 1)
    ]
    cuts = [(0, CUT), (CUT, width)]
    pieces = run(
        *(job(part(cut_kernel, a), [sds((n, b - a), bf16)], gr) for a, b in cuts),
        after=(mirrored, *weights),
    )
    flips = [flip(pieces[0][0])]
    flips.append(flip(lax.optimization_barrier((pieces[1][0], flips[0]))[0]))

    def part_job(backward, pieces, *arrays):
        body = part(part_kernel, backward, len(pieces))
        return job(body, part_shapes, *pieces, *arrays, scalars=(core,))

    def chip_job(upward, own, near):
        return job(part(chip_kernel, upward), chip_shapes, own, *near, scalars=(core,))

    ((held,),) = run(
        job(stack_kernel, [sds((chips, *local.shape), bf16)], *weights, mirrored[n + heads :])
    )
    ((early_own, *sends),) = run(
        part_job(True, [gr], mirrored[:n], mirrored[n : n + heads]), after=(held,)
    )
    early_near = [over_cores(send) for send in sends]
    ((right_own, *sends),) = run(part_job(False, [gf], read, decay))
    right_near = [over_cores(send) for send in sends]
    (early_term, early_decay), (read_r, rows, cols) = run(
        chip_job(False, early_own, early_near),
        job(
            tables_kernel,
            [
                sds((n, state), bf16),
                sds((5, heads, n), f32),
                sds((heads // GROUP, n, LANES), f32),
            ],
            read,
            decay,
            step,
        ),
        after=(right_own,),
    )
    earlies = []
    for i in range(span - 1):
        leaving = early_term
        if i:
            ((leaving,),) = run(
                job(onward_kernel, [half_shape], early_term, early_decay, *earlies)
            )
        earlies.append(over_chips(leaving, (chips - 1 - i, chips - 2 - i)))
    ((right_term, right_decay),) = run(
        chip_job(False, right_own, right_near), after=(early_term,)
    )
    rights = [over_chips(right_term, (chips - 1, chips - 2))]
    got = over_cores(held)
    ((held,),) = run(
        job(
            pair_kernel,
            [sds((chips, 2, *local.shape), bf16)],
            held,
            got,
            scalars=(chip, core),
        ),
        after=(right_term,),
    )
    held = held.reshape(-1, state)
    (shares,) = run(
        job(share_kernel, [sds((2 * share, n), bf16)] * dp_count, hidden, held, scalars=(dp,))
    )
    shared = [shares[0]] + [over_dp(shares[k], k) for k in range(1, dp_count)]
    ((mix_f,),) = run(
        job(part(mix_kernel, True, 1), [sds((n, n), f32)], gf, inner, rows[CUM2], cols),
        after=(right_term,),
    )
    right_far = over_cores(right_own)
    ((leaving,),) = run(
        job(onward_kernel, [half_shape], right_term, right_decay, *rights),
        after=(mix_f, right_far, *shared[1:4]),
    )
    rights.append(over_chips(leaving, (chips - 2, chips - 3)))

    ((left_own, *sends),) = run(part_job(True, flips, read, decay), after=(leaving,))
    left_near = [over_cores(send) for send in sends]
    lefts = []
    for i in range(span - 1):
        early = [] if i else [early_term, early_decay, *earlies]
        shapes = [half_shape] * (1 if i else 2)
        (leaving, *middle), = run(
            job(
                part(left_kernel, len(early)),
                shapes,
                left_own,
                *left_near,
                *early,
                *lefts,
                scalars=(core, chip == span),
            )
        )
        lefts += middle
        lefts.append(over_chips(leaving, (i, i + 1), (span + i, span + i + 1)))
    left_far = over_cores(left_own)
    for i in range(2, chips - 1):
        ((leaving,),) = run(
            job(onward_kernel, [half_shape], right_term, right_decay, *rights),
        )
        rights.append(over_chips(leaving, (chips - 1 - i, chips - 2 - i)))
    ((mix_b,),) = run(
        job(
            part(mix_kernel, False, len(flips)),
            [sds((n, n), f32)],
            *flips,
            inner,
            rows[EXCLR2],
            cols,
        ),
        after=(leaving,),
    )
    ((halves,),) = run(
        job(part(halves_kernel, len(rights)), [sds((state, width), bf16)], *rights, *lefts),
        after=(left_far, *shared[4:]),
    )
    swapped = over_cores(halves)

    ((right_in, left_in, grad_write),) = run(
        job(
            write_kernel,
            [sds((state, width), bf16), sds((state, width), bf16), sds((n, state), bf16)],
            inner,
            halves,
            swapped,
            right_far,
            left_far,
            rows,
            mix_f,
            mix_b,
            read,
            read_r,
            *right_near,
            *left_near,
            scalars=(core,),
        )
    )

    writes = [grad_write] + [over_dp(grad_write, k) for k in range(1, dp_count)]
    ((weight,),) = run(
        job(gather_kernel, [sds((dp_count, share, state), bf16)], *shared, scalars=(dp,)),
        after=(grad_write,),
    )
    weight = weight.reshape(-1, state)
    write = jnp.dot(hidden, weight, preferred_element_type=f32).astype(bf16)
    inner_arrays = (gf, right_in, left_in, rows, cols, write, read, read_r, *flips)
    half_inner = run_on_half(part(inner_kernel, 0), 0, sds((n, width), bf16), inner_arrays, ())
    piece = share // ctx_count
    ((keep, give),) = run(
        job(
            product_kernel,
            [sds((chips, piece, state), f32), sds((chips, piece, state), bf16)],
            *shared,
            *writes,
            scalars=(core,),
        ),
        after=(half_inner,),
    )
    ((total, *dealt),) = run(
        job(
            deal_kernel,
            [sds((piece, state), f32)] + [sds((piece, state), bf16)] * (chips - 1),
            keep,
            over_cores(give),
            scalars=(chip,),
        )
    )
    for k in range(1, chips):
        total = total + lax.ppermute(dealt[k - 1], "ctx", xor_pairs(ctx_count, 2 * k)).astype(f32)
    grad_weight = total / (dp_count * ctx_count * n)

    grad_inner = run_on_half(
        part(inner_kernel, 1), 1, sds((n, width), bf16), inner_arrays, (half_inner,), tuple(dealt[:1])
    )
    grad_hidden = dot_nt(grad_write, weight).astype(bf16)
    return grad_inner[None], grad_hidden[None], grad_weight


def solution(mesh):
    in_specs = (
        P("dp", "ctx", None),
        P(("dp", "ctx"), None),
        P(("dp", "ctx")),
        P("dp", "ctx", None),
        P("dp", "ctx", None),
        P("dp", None, "ctx"),
        P("dp", None, "ctx"),
        P("dp", "ctx", None),
        P("dp", "ctx", None),
    )
    out_specs = (P("dp", "ctx", None), P("dp", "ctx", None), P(("dp", "ctx"), None))
    return jax.shard_map(shards, mesh=mesh, in_specs=in_specs, out_specs=out_specs, check_vma=False)
```

```python
import functools
import itertools

import jax
import jax.numpy as jnp
from jax import lax
from jax.experimental import pallas as pl
from jax.experimental.pallas import tpu as pltpu
from jax.sharding import PartitionSpec as P

BLOCK = 128
LANES = 128
GROUP = 8
LOG2E = 1.4426950408889634
LOW = -1e30
EXACT = lax.Precision.HIGHEST
VMEM_BYTES = 9 * 1024 * 1024
CUT = 1024
PIECES = 2

f32 = jnp.float32
bf16 = jnp.bfloat16

CUM2, EXCLR2, FWD_EDGE, BACK_EDGE, STEP = range(5)
C_MIX_FWD, C_MIX_BACK, C_CUM2, C_EXCL2 = range(4)


def sds(shape, dtype):
    return jax.ShapeDtypeStruct(shape, dtype)


def job(body, outs, *arrays, scalars=()):
    return body, outs, arrays, [jnp.reshape(s, (1,)).astype(jnp.int32) for s in scalars]


def run(*jobs, after=(), flops=0):
    vmem = pl.BlockSpec(memory_space=pltpu.VMEM)
    smem = pl.BlockSpec(memory_space=pltpu.SMEM)
    ins, specs, outs, calls = [], [], [], []
    for body, job_outs, arrays, scalars in jobs:
        calls.append((body, len(ins), len(scalars) + len(arrays), len(outs), len(job_outs)))
        ins += [*scalars, *arrays]
        specs += [smem] * len(scalars) + [vmem] * len(arrays)
        outs += job_outs
    lead = len(ins)
    if after:
        ins[-1] = lax.optimization_barrier((ins[-1], *after))[0]

    def kernel(*refs):
        for body, i, ni, o, no in calls:
            body(*refs[i : i + ni], *refs[lead + o : lead + o + no])

    got = pl.pallas_call(
        kernel,
        out_shape=outs,
        in_specs=specs,
        out_specs=[vmem] * len(outs),
        compiler_params=pltpu.CompilerParams(vmem_limit_bytes=VMEM_BYTES),
        cost_estimate=pl.CostEstimate(flops=flops, transcendentals=0, bytes_accessed=flops // 250),
    )(*ins)
    return [list(got[o : o + no]) for _, _, _, o, no in calls]


def run_on_half(body, side, shape, scalar, arrays, before, after=()):
    vmem = pl.BlockSpec(memory_space=pltpu.VMEM)
    smem = pl.BlockSpec(memory_space=pltpu.SMEM)
    anywhere = pl.BlockSpec(memory_space=pl.ANY)
    rest = [*before]
    if after:
        arrays = [*arrays[:-1], lax.optimization_barrier((arrays[-1], *after))[0]]

    def kernel(*refs):
        body(*refs[: len(arrays) + 1], refs[-1])

    return pl.pallas_call(
        kernel,
        grid=(1,),
        out_shape=shape,
        in_specs=[smem] + [vmem] * len(arrays) + [anywhere] * len(rest),
        out_specs=pl.BlockSpec((shape.shape[0], shape.shape[1] // 2), lambda i: (0, side)),
        input_output_aliases={len(arrays) + 1: 0} if before else {},
        compiler_params=pltpu.CompilerParams(vmem_limit_bytes=VMEM_BYTES),
        cost_estimate=pl.CostEstimate(flops=0, transcendentals=0, bytes_accessed=0),
    )(jnp.reshape(scalar, (1,)).astype(jnp.int32), *arrays, *rest)


def iotas(shape):
    return lax.broadcasted_iota(jnp.int32, shape, 0), lax.broadcasted_iota(jnp.int32, shape, 1)


def dot_nt(a, b):
    return lax.dot_general(a, b, (((1,), (1,)), ((), ())), preferred_element_type=f32)


def dot_tn(a, b):
    return lax.dot_general(a, b, (((0,), (0,)), ((), ())), preferred_element_type=f32)


def spread(rows, width):
    high = rows.astype(bf16).astype(f32)
    both = jnp.concatenate([high, rows - high], axis=0).astype(bf16)
    r, c = iotas((2 * GROUP, GROUP * width))
    pick = (r % GROUP == c // width).astype(f32).astype(bf16)
    return dot_tn(both, pick)


def tables_kernel(read_ref, decay_ref, step_ref, readr_ref, rows_ref, cols_ref):
    decay = decay_ref[...]
    heads, n = decay.shape
    r, c = iotas((n, n))
    upto = (r <= c).astype(f32)
    flip = (r + c == n - 1).astype(f32)
    readr_ref[...] = jnp.dot(
        flip.astype(bf16), read_ref[...], preferred_element_type=f32
    ).astype(bf16)
    cum = jnp.dot(decay, upto, precision=EXACT, preferred_element_type=f32)
    decay_r = jnp.dot(decay, flip, precision=EXACT, preferred_element_type=f32)
    cum_r = jnp.dot(decay_r, upto, precision=EXACT, preferred_element_type=f32)
    end = cum[:, n - 1 :]
    excl = cum - decay
    step = step_ref[...]
    log_step = jnp.log(step) * LOG2E
    cum2 = cum * LOG2E
    excl2 = excl * LOG2E
    rows_ref[CUM2] = cum2
    rows_ref[EXCLR2] = (end - cum_r) * LOG2E
    rows_ref[FWD_EDGE] = step * jnp.exp(end - cum)
    rows_ref[BACK_EDGE] = step * jnp.exp(excl)
    rows_ref[STEP] = step
    planes = (cum2 - log_step, excl2 + log_step, cum2, excl2)
    rest = jnp.zeros((LANES - GROUP * len(planes), n), f32)
    for g in range(heads // GROUP):
        part = [p[g * GROUP : (g + 1) * GROUP] for p in planes]
        cols_ref[g] = jnp.concatenate(part + [rest], axis=0).T


def columns(refs, at, count, value=None):
    for ref in refs:
        if at < ref.shape[1]:
            if value is None:
                return ref[:, at : at + count]
            ref[:, at : at + count] = value
            return None
        at -= ref.shape[1]


def summed(lists, at, count):
    total = columns(lists[0], at, count)
    for refs in lists[1:]:
        total = total + columns(refs, at, count)
    return total


def split(refs, counts):
    lists = []
    for count in counts:
        lists.append(refs[:count])
        refs = refs[count:]
    return lists, refs


def part_kernel(backward, count, core_ref, *refs):
    g_refs, (read_ref, decay_ref, own_ref, *send_refs) = refs[:count], refs[count:]
    heads, n = decay_ref.shape
    width = sum(ref.shape[1] for ref in g_refs) // heads
    step = GROUP * width
    r, c = iotas((n, n))
    order = ((r + c == n - 1) if backward else (r == c)).astype(f32)
    upto = (r <= c).astype(f32)
    read_t = dot_tn(read_ref[...].astype(bf16), order.astype(bf16)).astype(bf16)
    decay = decay_ref[...]
    if backward:
        decay = jnp.dot(decay, order, precision=EXACT, preferred_element_type=f32)
    weight = jnp.exp(jnp.dot(decay, upto, precision=EXACT, preferred_element_type=f32))
    state = read_t.shape[0]
    groups = heads // GROUP
    tail_row, _ = iotas((16, step))
    low = core_ref[0] == 0

    def term_of(g):
        scale = spread(weight[g * GROUP : (g + 1) * GROUP], width)
        cotangent = columns(g_refs, g * step, step)
        scaled = (cotangent.astype(f32) * scale).astype(bf16)
        term = jnp.dot(read_t, scaled, preferred_element_type=f32)
        last = scale[n - 1 :]
        high = last.astype(bf16).astype(f32)
        tail = jnp.where(tail_row == 0, high, jnp.where(tail_row == 1, last - high, 0.0))
        return jnp.concatenate([term, tail], axis=0)

    for g in range(groups // 2):
        here = slice(g * step, (g + 1) * step)
        lower, upper = term_of(g), term_of(g + groups // 2)
        own_ref[:, here] = jnp.where(low, lower, upper).astype(bf16)
        sent = jnp.where(low, upper, lower).astype(bf16)
        columns(send_refs, g * step, step, sent)


WIDE = 512


def chip_terms(upward, core, own_ref, near_refs):
    state = own_ref.shape[0] - 16
    first = core == (0 if upward else 1)
    for c in range(own_ref.shape[1] // WIDE):
        here = slice(c * WIDE, (c + 1) * WIDE)
        own = own_ref[:, here].astype(f32)
        other = columns(near_refs, c * WIDE, WIDE).astype(f32)
        own_term, other_term = own[:state], other[:state]
        own_decay = own[state : state + 1] + own[state + 1 : state + 2]
        other_decay = other[state : state + 1] + other[state + 1 : state + 2]
        later = jnp.where(first, other_decay, own_decay)
        term = jnp.where(first, other_term, own_term) + later * jnp.where(
            first, own_term, other_term
        )
        yield here, term, own_decay * other_decay


def chip_kernel(upward, core_ref, own_ref, *refs):
    *near_refs, term_ref, decay_ref = refs
    for here, term, decay in chip_terms(upward, core_ref[0], own_ref, near_refs):
        term_ref[:, here] = term.astype(bf16)
        decay_ref[:, here] = decay


def entered(refs, here):
    state = refs[0][:, here].astype(f32)
    for ref in refs[1:]:
        state = state + ref[:, here].astype(f32)
    return state


def onward_kernel(term_ref, decay_ref, *refs):
    *entering, out_ref = refs
    for c in range(out_ref.shape[1] // WIDE):
        here = slice(c * WIDE, (c + 1) * WIDE)
        out_ref[:, here] = (
            term_ref[:, here].astype(f32) + decay_ref[:, here] * entered(entering, here)
        ).astype(bf16)


def middle_kernel(flag_ref, term_ref, decay_ref, *refs):
    *entering, out_ref = refs
    for c in range(out_ref.shape[1] // WIDE):
        here = slice(c * WIDE, (c + 1) * WIDE)
        leaving = term_ref[:, here].astype(f32)
        if entering:
            leaving = leaving + decay_ref[:, here] * entered(entering, here)
        out_ref[:, here] = jnp.where(flag_ref[0] == 1, leaving, 0.0).astype(bf16)


def left_kernel(count, core_ref, flag_ref, own_ref, *refs):
    near_refs, early, refs = refs[:PIECES], refs[PIECES : PIECES + count], refs[PIECES + count :]
    if early:
        out_ref, middle_ref = refs
        middle_kernel(flag_ref, *early, middle_ref)
        entering = [middle_ref]
    else:
        *entering, out_ref = refs
    for here, term, decay in chip_terms(True, core_ref[0], own_ref, near_refs):
        out_ref[:, here] = (term + decay * entered(entering, here)).astype(bf16)


def halves_kernel(count, *refs):
    rights, lefts, out_ref = refs[:count], refs[count:-1], refs[-1]
    half = out_ref.shape[1] // 2
    for c in range(half // WIDE):
        here = slice(c * WIDE, (c + 1) * WIDE)
        there = slice(half + c * WIDE, half + (c + 1) * WIDE)
        out_ref[:, here] = entered(rights, here).astype(bf16)
        out_ref[:, there] = entered(lefts, here).astype(bf16)


def mix_kernel(fwd, counts, *refs):
    lists, (inner_ref, row_ref, cols_ref, out_ref) = split(refs, counts)
    heads, n = row_ref.shape
    width = inner_ref.shape[1] // heads
    step = GROUP * width
    s, t = iotas((n, n))
    keep = (t >= s) if fwd else (t + s >= n - 1)
    low_half = t < width
    acc = jnp.zeros((n, n), f32)
    for g in range(heads // GROUP):
        rows = row_ref[g * GROUP : (g + 1) * GROUP]
        cols = cols_ref[g]
        for pair in range(GROUP // 2):
            at = g * step + pair * LANES
            inner = inner_ref[:, at : at + LANES].astype(f32)
            halves = jnp.concatenate(
                [jnp.where(low_half, inner, 0.0), jnp.where(low_half, 0.0, inner)], axis=0
            ).astype(bf16)
            dots = dot_nt(halves, summed(lists, at, LANES))
            for j in range(2):
                h = 2 * pair + j
                row = rows[h : h + 1]
                if fwd:
                    k = C_MIX_FWD * GROUP + h
                    power = row - cols[:, k : k + 1]
                else:
                    k = C_MIX_BACK * GROUP + h
                    power = cols[:, k : k + 1] - row
                decay = jnp.exp2(jnp.where(keep, power, LOW))
                acc = acc + decay * dots[j * n : (j + 1) * n]
    out_ref[...] = acc


def edge_terms(upward, own, core, inner_ref, half_ref, near_refs, far_ref, edge_ref, state_ref):
    heads, n = edge_ref.shape
    width = inner_ref.shape[1] // heads
    step = GROUP * width
    groups = heads // GROUP // 2
    first = core == (0 if upward else 1)
    rows = state_ref.shape[0]
    base = core if own else 1 - core
    at = groups * step if upward else 0
    acc = 0.0
    for g in range(groups):
        here = pl.ds(pl.multiple_of((base * groups + g) * step, step), step)
        heads_here = pl.ds(pl.multiple_of((base * groups + g) * GROUP, GROUP), GROUP)
        whole = half_ref[:, at + g * step : at + (g + 1) * step].astype(f32)
        other = columns(near_refs, g * step, step) if own else far_ref[:, g * step : (g + 1) * step]
        other = other.astype(f32)
        decay = other[rows : rows + 1] + other[rows + 1 : rows + 2]
        entering = jnp.where(first, whole, other[:rows] + decay * whole).astype(bf16)
        state_ref[:, g * step : (g + 1) * step] = entering
        scaled = inner_ref[:, here].astype(f32) * spread(edge_ref[heads_here], width)
        acc = acc + dot_nt(scaled.astype(bf16), entering)
    return acc


def own_kernel(
    core_ref, inner_ref, halves_ref, rows_ref, mixf_ref, mixb_ref, read_ref, readr_ref, *refs
):
    right_refs, left_refs = refs[:PIECES], refs[PIECES : 2 * PIECES]
    right_ref, left_ref, out_ref = refs[2 * PIECES :]
    acc = jnp.dot(mixf_ref[...].astype(bf16), read_ref[...], preferred_element_type=f32)
    acc = acc + jnp.dot(mixb_ref[...].astype(bf16), readr_ref[...], preferred_element_type=f32)
    for upward, near, plane, state_ref in (
        (False, right_refs, FWD_EDGE, right_ref),
        (True, left_refs, BACK_EDGE, left_ref),
    ):
        acc = acc + edge_terms(
            upward, True, core_ref[0], inner_ref, halves_ref, near, None, rows_ref.at[plane], state_ref
        )
    out_ref[...] = acc


def write_kernel(
    core_ref, inner_ref, swapped_ref, rows_ref, acc_ref, right_far_ref, left_far_ref, *refs
):
    right_ref, left_ref, out_ref = refs
    acc = acc_ref[...]
    for upward, far, plane, state_ref in (
        (False, right_far_ref, FWD_EDGE, right_ref),
        (True, left_far_ref, BACK_EDGE, left_ref),
    ):
        acc = acc + edge_terms(
            upward, False, core_ref[0], inner_ref, swapped_ref, None, far, rows_ref.at[plane], state_ref
        )
    out_ref[...] = acc.astype(bf16)


def share_kernel(dp_ref, hidden_ref, weight_ref, *out_refs):
    share = weight_ref.shape[0]
    for k, out_ref in enumerate(out_refs):
        for c in range(share // LANES):
            at = pl.multiple_of((dp_ref[0] ^ k) * share + c * LANES, LANES)
            out_ref[c * LANES : (c + 1) * LANES] = (
                hidden_ref[:, pl.ds(at, LANES)].astype(f32).T.astype(bf16)
            )
        out_ref[share:] = weight_ref[...]


def product_kernel(core_ref, *refs):
    count = (len(refs) - 2) // 2
    hidden_refs, write_refs = refs[:count], refs[count : 2 * count]
    keep_ref, give_ref = refs[2 * count :]
    chips, piece, _ = keep_ref.shape
    writes = [w[...] for w in write_refs]
    for which, out_ref in ((core_ref[0], keep_ref), (1 - core_ref[0], give_ref)):
        for chip in range(chips):
            rows = pl.ds(pl.multiple_of((2 * chip + which) * piece, piece), piece)
            total = jnp.dot(hidden_refs[0][rows], writes[0], preferred_element_type=f32)
            for k in range(1, count):
                total = total + jnp.dot(hidden_refs[k][rows], writes[k], preferred_element_type=f32)
            out_ref[chip] = total.astype(out_ref.dtype)


def deal_kernel(chip_ref, keep_ref, got_ref, own_ref, *out_refs):
    chip = chip_ref[0]
    own_ref[...] = keep_ref[chip] + got_ref[chip].astype(f32)
    for k, out_ref in enumerate(out_refs, 1):
        out_ref[...] = (keep_ref[chip ^ k] + got_ref[chip ^ k].astype(f32)).astype(bf16)


def cut_kernel(start, array_ref, out_ref):
    out_ref[...] = array_ref[:, start : start + out_ref.shape[1]]


def stack_kernel(*refs):
    *arrays, out_ref = refs
    for k, ref in enumerate(arrays):
        out_ref[k] = ref[...].astype(bf16)


def pair_kernel(chip_ref, core_ref, held_ref, got_ref, out_ref):
    chip, core = chip_ref[0], core_ref[0]
    chips = held_ref.shape[0]
    for k in range(chips):
        held_core = core if k < chips - 1 else 1 - core
        out_ref[chip ^ k, held_core] = held_ref[k]
        out_ref[chip ^ k, 1 - held_core] = got_ref[k]


def gather_kernel(index_ref, *refs):
    *arrays, out_ref = refs
    rows = out_ref.shape[1]
    for k, ref in enumerate(arrays):
        out_ref[index_ref[0] ^ k] = ref[ref.shape[0] - rows :]


def inner_kernel(
    side, core_ref, gf_ref, right_own_ref, right_rest_ref, left_own_ref, left_rest_ref, *refs
):
    rows_ref, cols_ref, write_ref, read_ref, readr_ref, *gb_refs, out_ref = refs
    own_side = core_ref[0] == side
    _, heads, n = rows_ref.shape
    width = gf_ref.shape[1] // heads
    step = GROUP * width
    half = heads // GROUP // 2
    write = write_ref[...]
    kernel_f = dot_nt(write, read_ref[...])
    kernel_b = dot_nt(write, readr_ref[...])
    s, t = iotas((n, n))
    low_half = t < width

    for g in range(side * half, (side + 1) * half):
        at = g * step
        own = slice(g * GROUP, (g + 1) * GROUP)
        half_at = at - side * half * step
        there = slice(half_at, half_at + step)
        cols = cols_ref[g]
        right = jnp.where(own_side, right_own_ref[:, there], right_rest_ref[:, there])
        left = jnp.where(own_side, left_own_ref[:, there], left_rest_ref[:, there])
        cum2 = rows_ref[CUM2, own]
        exclr2 = rows_ref[EXCLR2, own]
        step_e = spread(rows_ref[STEP, own], width)
        edges = spread(rows_ref[FWD_EDGE, own], width) * jnp.dot(
            write, right, preferred_element_type=f32
        )
        edges = edges + spread(rows_ref[BACK_EDGE, own], width) * jnp.dot(
            write, left, preferred_element_type=f32
        )
        for pair in range(GROUP // 2):
            mixes = []
            for j in range(2):
                h = 2 * pair + j
                kf = C_CUM2 * GROUP + h
                kb = C_EXCL2 * GROUP + h
                pf = cum2[h : h + 1] - cols[:, kf : kf + 1]
                pb = cols[:, kb : kb + 1] - exclr2[h : h + 1]
                mf = jnp.exp2(jnp.where(t >= s, pf, LOW)) * kernel_f
                mb = jnp.exp2(jnp.where(t + s >= n - 1, pb, LOW)) * kernel_b
                mixes.append(jnp.concatenate([mf, mb], axis=1))
            here = at + pair * LANES
            both = jnp.concatenate(
                [gf_ref[:, here : here + LANES], columns(gb_refs, here, LANES)], axis=0
            )
            got = jnp.dot(
                jnp.concatenate(mixes, axis=0).astype(bf16), both, preferred_element_type=f32
            )
            intra = jnp.where(low_half, got[:n], got[n:])
            mine = slice(pair * LANES, (pair + 1) * LANES)
            into = (g - side * half) * step + pair * LANES
            out_ref[:, into : into + LANES] = (step_e[:, mine] * intra + edges[:, mine]).astype(
                bf16
            )


def xor_pairs(count, k):
    return [(i, i ^ k) for i in range(count)]


def chip_pairs(moves):
    return [(2 * a + i, 2 * b + i) for a, b in moves for i in range(2)]


def shards(
    hidden_in,
    write_weight,
    shard_scale,
    inner_acts,
    read_proj,
    step_size,
    log_decay,
    grad_fwd,
    grad_rev,
):
    ctx_count = lax.axis_size("ctx")
    dp_count = lax.axis_size("dp")
    ctx = lax.axis_index("ctx")
    dp = lax.axis_index("dp")
    core, chip = ctx % 2, ctx // 2
    chips = ctx_count // 2
    span = chips // 2
    hidden = hidden_in[0]
    inner = inner_acts[0]
    read = read_proj[0]
    step = step_size[0]
    decay = log_decay[0]
    gf = grad_fwd[0]
    gr = grad_rev[0]
    n, width = inner.shape
    heads = decay.shape[0]
    state = read.shape[1]
    half = width // 2
    share = hidden.shape[1] // dp_count
    part = functools.partial
    part_shapes = [sds((state + 16, half), bf16)]
    part_shapes += [sds((state + 16, half // PIECES), bf16)] * PIECES
    half_shape = sds((state, half), bf16)
    chip_shapes = [half_shape, sds((1, half), f32)]

    def over_cores(array):
        return lax.ppermute(array, "ctx", xor_pairs(ctx_count, 1))

    def over_chips(array, *moves):
        return lax.ppermute(array, "ctx", chip_pairs(moves))

    def over_dp(array, k):
        return lax.ppermute(array, "dp", xor_pairs(dp_count, k))

    def flip(piece):
        return lax.ppermute(piece, "ctx", [(i, ctx_count - 1 - i) for i in range(ctx_count)])

    local = (write_weight.astype(f32) * shard_scale[0]).astype(bf16)
    mirrored = flip(jnp.concatenate([read.astype(f32), decay, local.astype(f32)], axis=0))
    weights = [local] + [
        lax.ppermute(local, "ctx", xor_pairs(ctx_count, 2 * k)) for k in range(1, chips - 1)
    ]
    cuts = [(0, CUT), (CUT, width)]
    pieces = run(
        *(job(part(cut_kernel, a), [sds((n, b - a), bf16)], gr) for a, b in cuts),
        after=(mirrored, *weights),
    )
    flips = [flip(pieces[0][0])]
    flips.append(flip(lax.optimization_barrier((pieces[1][0], flips[0]))[0]))

    def part_job(backward, pieces, *arrays):
        body = part(part_kernel, backward, len(pieces))
        return job(body, part_shapes, *pieces, *arrays, scalars=(core,))

    def chip_job(upward, own, near):
        return job(part(chip_kernel, upward), chip_shapes, own, *near, scalars=(core,))

    ((held,),) = run(
        job(stack_kernel, [sds((chips, *local.shape), bf16)], *weights, mirrored[n + heads :])
    )
    ((early_own, *sends),) = run(
        part_job(True, [gr], mirrored[:n], mirrored[n : n + heads]), after=(held,)
    )
    early_near = [over_cores(send) for send in sends]
    ((right_own, *sends),) = run(part_job(False, [gf], read, decay))
    right_near = [over_cores(send) for send in sends]
    (early_term, early_decay), (read_r, rows, cols) = run(
        chip_job(False, early_own, early_near),
        job(
            tables_kernel,
            [
                sds((n, state), bf16),
                sds((5, heads, n), f32),
                sds((heads // GROUP, n, LANES), f32),
            ],
            read,
            decay,
            step,
        ),
        after=(right_own,),
    )
    earlies = []
    for i in range(span - 1):
        leaving = early_term
        if i:
            ((leaving,),) = run(
                job(onward_kernel, [half_shape], early_term, early_decay, *earlies)
            )
        earlies.append(over_chips(leaving, (chips - 1 - i, chips - 2 - i)))
    ((right_term, right_decay),) = run(
        chip_job(False, right_own, right_near), after=(early_term,)
    )
    rights = [over_chips(right_term, (chips - 1, chips - 2))]
    got = over_cores(held)
    ((held,),) = run(
        job(
            pair_kernel,
            [sds((chips, 2, *local.shape), bf16)],
            held,
            got,
            scalars=(chip, core),
        ),
        after=(right_term,),
    )
    held = held.reshape(-1, state)
    (shares,) = run(
        job(share_kernel, [sds((2 * share, n), bf16)] * dp_count, hidden, held, scalars=(dp,))
    )
    shared = [shares[0]] + [over_dp(shares[k], k) for k in range(1, dp_count)]
    ((mix_f,),) = run(
        job(part(mix_kernel, True, [1]), [sds((n, n), f32)], gf, inner, rows[CUM2], cols),
        after=(right_term,),
    )
    right_far = over_cores(right_own)
    ((leaving,),) = run(
        job(onward_kernel, [half_shape], right_term, right_decay, *rights),
        after=(mix_f, right_far, *shared[1:4]),
    )
    rights.append(over_chips(leaving, (chips - 2, chips - 3)))

    ((left_own, *sends),) = run(part_job(True, flips, read, decay), after=(leaving,))
    left_near = [over_cores(send) for send in sends]
    lefts = []
    for i in range(span - 1):
        early = [] if i else [early_term, early_decay, *earlies]
        shapes = [half_shape] * (1 if i else 2)
        (leaving, *middle), = run(
            job(
                part(left_kernel, len(early)),
                shapes,
                left_own,
                *left_near,
                *early,
                *lefts,
                scalars=(core, chip == span),
            )
        )
        lefts += middle
        lefts.append(over_chips(leaving, (i, i + 1), (span + i, span + i + 1)))
    left_far = over_cores(left_own)
    for i in range(2, chips - 1):
        ((leaving,),) = run(
            job(onward_kernel, [half_shape], right_term, right_decay, *rights),
        )
        rights.append(over_chips(leaving, (chips - 1 - i, chips - 2 - i)))
    ((mix_b,),) = run(
        job(
            part(mix_kernel, False, [len(flips)]),
            [sds((n, n), f32)],
            *flips,
            inner,
            rows[EXCLR2],
            cols,
        ),
        after=(leaving,),
    )
    ((halves,),) = run(
        job(part(halves_kernel, len(rights)), [sds((state, width), bf16)], *rights, *lefts),
        after=(left_far, mix_b, *shared[4:]),
    )
    swapped = over_cores(halves)

    ((right_own_in, left_own_in, own_write),) = run(
        job(
            own_kernel,
            [half_shape, half_shape, sds((n, state), f32)],
            inner,
            halves,
            rows,
            mix_f,
            mix_b,
            read,
            read_r,
            *right_near,
            *left_near,
            scalars=(core,),
        )
    )
    ((right_rest_in, left_rest_in, grad_write),) = run(
        job(
            write_kernel,
            [half_shape, half_shape, sds((n, state), bf16)],
            inner,
            swapped,
            rows,
            own_write,
            right_far,
            left_far,
            scalars=(core,),
        )
    )

    writes = [grad_write] + [over_dp(grad_write, k) for k in range(1, dp_count)]
    ((weight,),) = run(
        job(gather_kernel, [sds((dp_count, share, state), bf16)], *shared, scalars=(dp,)),
        after=(grad_write,),
    )
    weight = weight.reshape(-1, state)
    write = jnp.dot(hidden, weight, preferred_element_type=f32).astype(bf16)
    entering = (right_own_in, right_rest_in, left_own_in, left_rest_in)
    inner_arrays = (gf, *entering, rows, cols, write, read, read_r, *flips)
    half_inner = run_on_half(part(inner_kernel, 0), 0, sds((n, width), bf16), core, inner_arrays, ())
    piece = share // ctx_count
    ((keep, give),) = run(
        job(
            product_kernel,
            [sds((chips, piece, state), f32), sds((chips, piece, state), bf16)],
            *shared,
            *writes,
            scalars=(core,),
        ),
        after=(half_inner,),
    )
    ((total, *dealt),) = run(
        job(
            deal_kernel,
            [sds((piece, state), f32)] + [sds((piece, state), bf16)] * (chips - 1),
            keep,
            over_cores(give),
            scalars=(chip,),
        )
    )
    for k in range(1, chips):
        total = total + lax.ppermute(dealt[k - 1], "ctx", xor_pairs(ctx_count, 2 * k)).astype(f32)
    grad_weight = total / (dp_count * ctx_count * n)

    grad_inner = run_on_half(
        part(inner_kernel, 1), 1, sds((n, width), bf16), core, inner_arrays, (half_inner,), tuple(dealt[:1])
    )
    grad_hidden = dot_nt(grad_write, weight).astype(bf16)
    return grad_inner[None], grad_hidden[None], grad_weight


def solution(mesh):
    in_specs = (
        P("dp", "ctx", None),
        P(("dp", "ctx"), None),
        P(("dp", "ctx")),
        P("dp", "ctx", None),
        P("dp", "ctx", None),
        P("dp", None, "ctx"),
        P("dp", None, "ctx"),
        P("dp", "ctx", None),
        P("dp", "ctx", None),
    )
    out_specs = (P("dp", "ctx", None), P("dp", "ctx", None), P(("dp", "ctx"), None))
    return jax.shard_map(shards, mesh=mesh, in_specs=in_specs, out_specs=out_specs, check_vma=False)
```

```python
import functools
import itertools

import jax
import jax.numpy as jnp
from jax import lax
from jax.experimental import pallas as pl
from jax.experimental.pallas import tpu as pltpu
from jax.sharding import PartitionSpec as P

BLOCK = 128
LANES = 128
GROUP = 8
LOG2E = 1.4426950408889634
LOW = -1e30
EXACT = lax.Precision.HIGHEST
VMEM_BYTES = 8 * 1024 * 1024
COSTLY = 10**10
CUT = 1024
PIECES = 2

f32 = jnp.float32
bf16 = jnp.bfloat16

CUM2, EXCLR2, FWD_EDGE, BACK_EDGE, STEP, BACK_WEIGHT = range(6)
C_MIX_FWD, C_MIX_BACK, C_CUM2, C_EXCL2 = range(4)


def sds(shape, dtype):
    return jax.ShapeDtypeStruct(shape, dtype)


def job(body, outs, *arrays, scalars=()):
    return body, outs, arrays, [jnp.reshape(s, (1,)).astype(jnp.int32) for s in scalars]


def run(*jobs, after=(), flops=0):
    vmem = pl.BlockSpec(memory_space=pltpu.VMEM)
    smem = pl.BlockSpec(memory_space=pltpu.SMEM)
    ins, specs, outs, calls = [], [], [], []
    for body, job_outs, arrays, scalars in jobs:
        calls.append((body, len(ins), len(scalars) + len(arrays), len(outs), len(job_outs)))
        ins += [*scalars, *arrays]
        specs += [smem] * len(scalars) + [vmem] * len(arrays)
        outs += job_outs
    lead = len(ins)
    if after:
        ins[-1] = lax.optimization_barrier((ins[-1], *after))[0]

    def kernel(*refs):
        for body, i, ni, o, no in calls:
            body(*refs[i : i + ni], *refs[lead + o : lead + o + no])

    got = pl.pallas_call(
        kernel,
        out_shape=outs,
        in_specs=specs,
        out_specs=[vmem] * len(outs),
        compiler_params=pltpu.CompilerParams(vmem_limit_bytes=VMEM_BYTES),
        cost_estimate=pl.CostEstimate(flops=flops, transcendentals=0, bytes_accessed=flops // 250),
    )(*ins)
    return [list(got[o : o + no]) for _, _, _, o, no in calls]


def run_on_half(body, side, shape, scalar, arrays, before, after=()):
    vmem = pl.BlockSpec(memory_space=pltpu.VMEM)
    smem = pl.BlockSpec(memory_space=pltpu.SMEM)
    anywhere = pl.BlockSpec(memory_space=pl.ANY)
    rest = [*before]
    if after:
        arrays = [*arrays[:-1], lax.optimization_barrier((arrays[-1], *after))[0]]

    def kernel(*refs):
        body(*refs[: len(arrays) + 1], refs[-1])

    return pl.pallas_call(
        kernel,
        grid=(1,),
        out_shape=shape,
        in_specs=[smem] + [vmem] * len(arrays) + [anywhere] * len(rest),
        out_specs=pl.BlockSpec((shape.shape[0], shape.shape[1] // 2), lambda i: (0, side)),
        input_output_aliases={len(arrays) + 1: 0} if before else {},
        compiler_params=pltpu.CompilerParams(vmem_limit_bytes=VMEM_BYTES),
        cost_estimate=pl.CostEstimate(flops=0, transcendentals=0, bytes_accessed=0),
    )(jnp.reshape(scalar, (1,)).astype(jnp.int32), *arrays, *rest)


def iotas(shape):
    return lax.broadcasted_iota(jnp.int32, shape, 0), lax.broadcasted_iota(jnp.int32, shape, 1)


def dot_nt(a, b):
    return lax.dot_general(a, b, (((1,), (1,)), ((), ())), preferred_element_type=f32)


def dot_tn(a, b):
    return lax.dot_general(a, b, (((0,), (0,)), ((), ())), preferred_element_type=f32)


def spread(rows, width):
    high = rows.astype(bf16).astype(f32)
    both = jnp.concatenate([high, rows - high], axis=0).astype(bf16)
    r, c = iotas((2 * GROUP, GROUP * width))
    pick = (r % GROUP == c // width).astype(f32).astype(bf16)
    return dot_tn(both, pick)


def tables_kernel(read_ref, decay_ref, step_ref, readr_ref, readt_ref, rows_ref, cols_ref):
    decay = decay_ref[...]
    heads, n = decay.shape
    r, c = iotas((n, n))
    upto = (r <= c).astype(f32)
    flip = (r + c == n - 1).astype(f32)
    readr_ref[...] = jnp.dot(
        flip.astype(bf16), read_ref[...], preferred_element_type=f32
    ).astype(bf16)
    readt_ref[...] = dot_tn(read_ref[...], flip.astype(bf16)).astype(bf16)
    cum = jnp.dot(decay, upto, precision=EXACT, preferred_element_type=f32)
    decay_r = jnp.dot(decay, flip, precision=EXACT, preferred_element_type=f32)
    cum_r = jnp.dot(decay_r, upto, precision=EXACT, preferred_element_type=f32)
    end = cum[:, n - 1 :]
    excl = cum - decay
    step = step_ref[...]
    log_step = jnp.log(step) * LOG2E
    cum2 = cum * LOG2E
    excl2 = excl * LOG2E
    rows_ref[CUM2] = cum2
    rows_ref[EXCLR2] = (end - cum_r) * LOG2E
    rows_ref[FWD_EDGE] = step * jnp.exp(end - cum)
    rows_ref[BACK_EDGE] = step * jnp.exp(excl)
    rows_ref[STEP] = step
    rows_ref[BACK_WEIGHT] = jnp.exp(cum_r)
    planes = (cum2 - log_step, excl2 + log_step, cum2, excl2)
    rest = jnp.zeros((LANES - GROUP * len(planes), n), f32)
    for g in range(heads // GROUP):
        part = [p[g * GROUP : (g + 1) * GROUP] for p in planes]
        cols_ref[g] = jnp.concatenate(part + [rest], axis=0).T


def columns(refs, at, count, value=None):
    for ref in refs:
        if at < ref.shape[1]:
            if value is None:
                return ref[:, at : at + count]
            ref[:, at : at + count] = value
            return None
        at -= ref.shape[1]


def summed(lists, at, count):
    total = columns(lists[0], at, count)
    for refs in lists[1:]:
        total = total + columns(refs, at, count)
    return total


def split(refs, counts):
    lists = []
    for count in counts:
        lists.append(refs[:count])
        refs = refs[count:]
    return lists, refs


def part_kernel(backward, count, core_ref, *refs):
    g_refs, (read_ref, decay_ref, own_ref, *send_refs) = refs[:count], refs[count:]
    heads, n = decay_ref.shape
    width = sum(ref.shape[1] for ref in g_refs) // heads
    step = GROUP * width
    if backward is None:
        read_t, weight = read_ref[...], decay_ref[...]
    else:
        r, c = iotas((n, n))
        order = ((r + c == n - 1) if backward else (r == c)).astype(f32)
        upto = (r <= c).astype(f32)
        read_t = dot_tn(read_ref[...].astype(bf16), order.astype(bf16)).astype(bf16)
        decay = decay_ref[...]
        if backward:
            decay = jnp.dot(decay, order, precision=EXACT, preferred_element_type=f32)
        weight = jnp.exp(jnp.dot(decay, upto, precision=EXACT, preferred_element_type=f32))
    state = read_t.shape[0]
    groups = heads // GROUP
    tail_row, _ = iotas((16, step))
    low = core_ref[0] == 0

    def term_of(g):
        scale = spread(weight[g * GROUP : (g + 1) * GROUP], width)
        cotangent = columns(g_refs, g * step, step)
        scaled = (cotangent.astype(f32) * scale).astype(bf16)
        term = jnp.dot(read_t, scaled, preferred_element_type=f32)
        last = scale[n - 1 :]
        high = last.astype(bf16).astype(f32)
        tail = jnp.where(tail_row == 0, high, jnp.where(tail_row == 1, last - high, 0.0))
        return jnp.concatenate([term, tail], axis=0)

    for g in range(groups // 2):
        here = slice(g * step, (g + 1) * step)
        lower, upper = term_of(g), term_of(g + groups // 2)
        own_ref[:, here] = jnp.where(low, lower, upper).astype(bf16)
        sent = jnp.where(low, upper, lower).astype(bf16)
        columns(send_refs, g * step, step, sent)


WIDE = 512


def chip_terms(upward, core, own_ref, near_refs):
    state = own_ref.shape[0] - 16
    first = core == (0 if upward else 1)
    for c in range(own_ref.shape[1] // WIDE):
        here = slice(c * WIDE, (c + 1) * WIDE)
        own = own_ref[:, here].astype(f32)
        other = columns(near_refs, c * WIDE, WIDE).astype(f32)
        own_term, other_term = own[:state], other[:state]
        own_decay = own[state : state + 1] + own[state + 1 : state + 2]
        other_decay = other[state : state + 1] + other[state + 1 : state + 2]
        later = jnp.where(first, other_decay, own_decay)
        term = jnp.where(first, other_term, own_term) + later * jnp.where(
            first, own_term, other_term
        )
        yield here, term, own_decay * other_decay


def chip_kernel(upward, core_ref, own_ref, *refs):
    *near_refs, term_ref, decay_ref = refs
    for here, term, decay in chip_terms(upward, core_ref[0], own_ref, near_refs):
        term_ref[:, here] = term.astype(bf16)
        decay_ref[:, here] = decay


def entered(refs, here):
    state = refs[0][:, here].astype(f32)
    for ref in refs[1:]:
        state = state + ref[:, here].astype(f32)
    return state


def onward_kernel(term_ref, decay_ref, *refs):
    *entering, out_ref = refs
    for c in range(out_ref.shape[1] // WIDE):
        here = slice(c * WIDE, (c + 1) * WIDE)
        out_ref[:, here] = (
            term_ref[:, here].astype(f32) + decay_ref[:, here] * entered(entering, here)
        ).astype(bf16)


def middle_kernel(flag_ref, term_ref, decay_ref, *refs):
    *entering, out_ref = refs
    for c in range(out_ref.shape[1] // WIDE):
        here = slice(c * WIDE, (c + 1) * WIDE)
        leaving = term_ref[:, here].astype(f32)
        if entering:
            leaving = leaving + decay_ref[:, here] * entered(entering, here)
        out_ref[:, here] = jnp.where(flag_ref[0] == 1, leaving, 0.0).astype(bf16)


def left_kernel(count, core_ref, flag_ref, own_ref, *refs):
    near_refs, early, refs = refs[:PIECES], refs[PIECES : PIECES + count], refs[PIECES + count :]
    if early:
        out_ref, middle_ref = refs
        middle_kernel(flag_ref, *early, middle_ref)
        entering = [middle_ref]
    else:
        *entering, out_ref = refs
    for here, term, decay in chip_terms(True, core_ref[0], own_ref, near_refs):
        out_ref[:, here] = (term + decay * entered(entering, here)).astype(bf16)


def halves_kernel(count, *refs):
    rights, lefts, out_ref = refs[:count], refs[count:-1], refs[-1]
    half = out_ref.shape[1] // 2
    for c in range(half // WIDE):
        here = slice(c * WIDE, (c + 1) * WIDE)
        there = slice(half + c * WIDE, half + (c + 1) * WIDE)
        out_ref[:, here] = entered(rights, here).astype(bf16)
        out_ref[:, there] = entered(lefts, here).astype(bf16)


def mix_kernel(fwd, counts, *refs):
    lists, (inner_ref, row_ref, cols_ref, out_ref) = split(refs, counts)
    heads, n = row_ref.shape
    width = inner_ref.shape[1] // heads
    step = GROUP * width
    s, t = iotas((n, n))
    keep = (t >= s) if fwd else (t + s >= n - 1)
    low_half = t < width
    acc = jnp.zeros((n, n), f32)
    for g in range(heads // GROUP):
        rows = row_ref[g * GROUP : (g + 1) * GROUP]
        cols = cols_ref[g]
        for pair in range(GROUP // 2):
            at = g * step + pair * LANES
            inner = inner_ref[:, at : at + LANES].astype(f32)
            halves = jnp.concatenate(
                [jnp.where(low_half, inner, 0.0), jnp.where(low_half, 0.0, inner)], axis=0
            ).astype(bf16)
            dots = dot_nt(halves, summed(lists, at, LANES))
            for j in range(2):
                h = 2 * pair + j
                row = rows[h : h + 1]
                if fwd:
                    k = C_MIX_FWD * GROUP + h
                    power = row - cols[:, k : k + 1]
                else:
                    k = C_MIX_BACK * GROUP + h
                    power = cols[:, k : k + 1] - row
                decay = jnp.exp2(jnp.where(keep, power, LOW))
                acc = acc + decay * dots[j * n : (j + 1) * n]
    out_ref[...] = acc


def edge_terms(upward, own, core, inner_ref, half_ref, near_refs, far_ref, edge_ref, state_ref):
    heads, n = edge_ref.shape
    width = inner_ref.shape[1] // heads
    step = GROUP * width
    groups = heads // GROUP // 2
    first = core == (0 if upward else 1)
    rows = state_ref.shape[0]
    base = core if own else 1 - core
    at = groups * step if upward else 0
    acc = 0.0
    for g in range(groups):
        here = pl.ds(pl.multiple_of((base * groups + g) * step, step), step)
        heads_here = pl.ds(pl.multiple_of((base * groups + g) * GROUP, GROUP), GROUP)
        whole = half_ref[:, at + g * step : at + (g + 1) * step].astype(f32)
        other = columns(near_refs, g * step, step) if own else far_ref[:, g * step : (g + 1) * step]
        other = other.astype(f32)
        decay = other[rows : rows + 1] + other[rows + 1 : rows + 2]
        entering = jnp.where(first, whole, other[:rows] + decay * whole).astype(bf16)
        state_ref[:, g * step : (g + 1) * step] = entering
        scaled = inner_ref[:, here].astype(f32) * spread(edge_ref[heads_here], width)
        acc = acc + dot_nt(scaled.astype(bf16), entering)
    return acc


def own_kernel(
    core_ref, inner_ref, halves_ref, rows_ref, mixf_ref, mixb_ref, read_ref, readr_ref, *refs
):
    right_refs, left_refs = refs[:PIECES], refs[PIECES : 2 * PIECES]
    right_ref, left_ref, out_ref = refs[2 * PIECES :]
    acc = jnp.dot(mixf_ref[...].astype(bf16), read_ref[...], preferred_element_type=f32)
    acc = acc + jnp.dot(mixb_ref[...].astype(bf16), readr_ref[...], preferred_element_type=f32)
    for upward, near, plane, state_ref in (
        (False, right_refs, FWD_EDGE, right_ref),
        (True, left_refs, BACK_EDGE, left_ref),
    ):
        acc = acc + edge_terms(
            upward, True, core_ref[0], inner_ref, halves_ref, near, None, rows_ref.at[plane], state_ref
        )
    out_ref[...] = acc


def write_kernel(
    core_ref, inner_ref, swapped_ref, rows_ref, acc_ref, right_far_ref, left_far_ref, *refs
):
    right_ref, left_ref, out_ref = refs
    acc = acc_ref[...]
    for upward, far, plane, state_ref in (
        (False, right_far_ref, FWD_EDGE, right_ref),
        (True, left_far_ref, BACK_EDGE, left_ref),
    ):
        acc = acc + edge_terms(
            upward, False, core_ref[0], inner_ref, swapped_ref, None, far, rows_ref.at[plane], state_ref
        )
    out_ref[...] = acc.astype(bf16)


def share_kernel(dp_ref, hidden_ref, weight_ref, *out_refs):
    share = weight_ref.shape[0]
    for k, out_ref in enumerate(out_refs):
        for c in range(share // LANES):
            at = pl.multiple_of((dp_ref[0] ^ k) * share + c * LANES, LANES)
            out_ref[c * LANES : (c + 1) * LANES] = (
                hidden_ref[:, pl.ds(at, LANES)].astype(f32).T.astype(bf16)
            )
        out_ref[share:] = weight_ref[...]


def product_kernel(core_ref, *refs):
    count = (len(refs) - 2) // 2
    hidden_refs, write_refs = refs[:count], refs[count : 2 * count]
    keep_ref, give_ref = refs[2 * count :]
    chips, piece, _ = keep_ref.shape
    writes = [w[...] for w in write_refs]
    for which, out_ref in ((core_ref[0], keep_ref), (1 - core_ref[0], give_ref)):
        for chip in range(chips):
            rows = pl.ds(pl.multiple_of((2 * chip + which) * piece, piece), piece)
            total = jnp.dot(hidden_refs[0][rows], writes[0], preferred_element_type=f32)
            for k in range(1, count):
                total = total + jnp.dot(hidden_refs[k][rows], writes[k], preferred_element_type=f32)
            out_ref[chip] = total.astype(out_ref.dtype)


def deal_kernel(chip_ref, keep_ref, got_ref, own_ref, *out_refs):
    chip = chip_ref[0]
    own_ref[...] = keep_ref[chip] + got_ref[chip].astype(f32)
    for k, out_ref in enumerate(out_refs, 1):
        out_ref[...] = (keep_ref[chip ^ k] + got_ref[chip ^ k].astype(f32)).astype(bf16)


def cut_kernel(start, array_ref, out_ref):
    out_ref[...] = array_ref[:, start : start + out_ref.shape[1]]


def stack_kernel(*refs):
    *arrays, out_ref = refs
    for k, ref in enumerate(arrays):
        out_ref[k] = ref[...].astype(bf16)


def pair_kernel(chip_ref, core_ref, held_ref, got_ref, out_ref):
    chip, core = chip_ref[0], core_ref[0]
    chips = held_ref.shape[0]
    for k in range(chips):
        held_core = core if k < chips - 1 else 1 - core
        out_ref[chip ^ k, held_core] = held_ref[k]
        out_ref[chip ^ k, 1 - held_core] = got_ref[k]


def gather_kernel(index_ref, *refs):
    *arrays, out_ref = refs
    rows = out_ref.shape[1]
    for k, ref in enumerate(arrays):
        out_ref[index_ref[0] ^ k] = ref[ref.shape[0] - rows :]


def inner_kernel(
    side, core_ref, gf_ref, right_own_ref, right_rest_ref, left_own_ref, left_rest_ref, *refs
):
    rows_ref, cols_ref, write_ref, read_ref, readr_ref, *gb_refs, out_ref = refs
    own_side = core_ref[0] == side
    _, heads, n = rows_ref.shape
    width = gf_ref.shape[1] // heads
    step = GROUP * width
    half = heads // GROUP // 2
    write = write_ref[...]
    kernel_f = dot_nt(write, read_ref[...])
    kernel_b = dot_nt(write, readr_ref[...])
    s, t = iotas((n, n))
    low_half = t < width

    for g in range(side * half, (side + 1) * half):
        at = g * step
        own = slice(g * GROUP, (g + 1) * GROUP)
        half_at = at - side * half * step
        there = slice(half_at, half_at + step)
        cols = cols_ref[g]
        right = jnp.where(own_side, right_own_ref[:, there], right_rest_ref[:, there])
        left = jnp.where(own_side, left_own_ref[:, there], left_rest_ref[:, there])
        cum2 = rows_ref[CUM2, own]
        exclr2 = rows_ref[EXCLR2, own]
        step_e = spread(rows_ref[STEP, own], width)
        edges = spread(rows_ref[FWD_EDGE, own], width) * jnp.dot(
            write, right, preferred_element_type=f32
        )
        edges = edges + spread(rows_ref[BACK_EDGE, own], width) * jnp.dot(
            write, left, preferred_element_type=f32
        )
        for pair in range(GROUP // 2):
            mixes = []
            for j in range(2):
                h = 2 * pair + j
                kf = C_CUM2 * GROUP + h
                kb = C_EXCL2 * GROUP + h
                pf = cum2[h : h + 1] - cols[:, kf : kf + 1]
                pb = cols[:, kb : kb + 1] - exclr2[h : h + 1]
                mf = jnp.exp2(jnp.where(t >= s, pf, LOW)) * kernel_f
                mb = jnp.exp2(jnp.where(t + s >= n - 1, pb, LOW)) * kernel_b
                mixes.append(jnp.concatenate([mf, mb], axis=1))
            here = at + pair * LANES
            both = jnp.concatenate(
                [gf_ref[:, here : here + LANES], columns(gb_refs, here, LANES)], axis=0
            )
            got = jnp.dot(
                jnp.concatenate(mixes, axis=0).astype(bf16), both, preferred_element_type=f32
            )
            intra = jnp.where(low_half, got[:n], got[n:])
            mine = slice(pair * LANES, (pair + 1) * LANES)
            into = (g - side * half) * step + pair * LANES
            out_ref[:, into : into + LANES] = (step_e[:, mine] * intra + edges[:, mine]).astype(
                bf16
            )


def xor_pairs(count, k):
    return [(i, i ^ k) for i in range(count)]


def chip_pairs(moves):
    return [(2 * a + i, 2 * b + i) for a, b in moves for i in range(2)]


def shards(
    hidden_in,
    write_weight,
    shard_scale,
    inner_acts,
    read_proj,
    step_size,
    log_decay,
    grad_fwd,
    grad_rev,
):
    ctx_count = lax.axis_size("ctx")
    dp_count = lax.axis_size("dp")
    ctx = lax.axis_index("ctx")
    dp = lax.axis_index("dp")
    core, chip = ctx % 2, ctx // 2
    chips = ctx_count // 2
    span = chips // 2
    hidden = hidden_in[0]
    inner = inner_acts[0]
    read = read_proj[0]
    step = step_size[0]
    decay = log_decay[0]
    gf = grad_fwd[0]
    gr = grad_rev[0]
    n, width = inner.shape
    heads = decay.shape[0]
    state = read.shape[1]
    half = width // 2
    share = hidden.shape[1] // dp_count
    part = functools.partial
    part_shapes = [sds((state + 16, half), bf16)]
    part_shapes += [sds((state + 16, half // PIECES), bf16)] * PIECES
    half_shape = sds((state, half), bf16)
    chip_shapes = [half_shape, sds((1, half), f32)]

    def over_cores(array):
        return lax.ppermute(array, "ctx", xor_pairs(ctx_count, 1))

    def over_chips(array, *moves):
        return lax.ppermute(array, "ctx", chip_pairs(moves))

    def over_dp(array, k):
        return lax.ppermute(array, "dp", xor_pairs(dp_count, k))

    def flip(piece):
        return lax.ppermute(piece, "ctx", [(i, ctx_count - 1 - i) for i in range(ctx_count)])

    local = (write_weight.astype(f32) * shard_scale[0]).astype(bf16)
    mirrored = flip(jnp.concatenate([read.astype(f32), decay, local.astype(f32)], axis=0))
    weights = [local] + [
        lax.ppermute(local, "ctx", xor_pairs(ctx_count, 2 * k)) for k in range(1, chips - 1)
    ]
    cuts = [(0, CUT), (CUT, width)]
    pieces = run(
        *(job(part(cut_kernel, a), [sds((n, b - a), bf16)], gr) for a, b in cuts),
        after=(mirrored, *weights),
    )
    flips = [flip(pieces[0][0])]
    flips.append(flip(lax.optimization_barrier((pieces[1][0], flips[0]))[0]))

    def part_job(backward, pieces, *arrays):
        body = part(part_kernel, backward, len(pieces))
        return job(body, part_shapes, *pieces, *arrays, scalars=(core,))

    def chip_job(upward, own, near):
        return job(part(chip_kernel, upward), chip_shapes, own, *near, scalars=(core,))

    ((held,),) = run(
        job(stack_kernel, [sds((chips, *local.shape), bf16)], *weights, mirrored[n + heads :])
    )
    ((early_own, *sends),) = run(
        part_job(True, [gr], mirrored[:n], mirrored[n : n + heads]), after=(held,)
    )
    early_near = [over_cores(send) for send in sends]
    ((right_own, *sends),) = run(part_job(False, [gf], read, decay))
    right_near = [over_cores(send) for send in sends]
    (early_term, early_decay), (read_r, read_t, rows, cols) = run(
        chip_job(False, early_own, early_near),
        job(
            tables_kernel,
            [
                sds((n, state), bf16),
                sds((state, n), bf16),
                sds((6, heads, n), f32),
                sds((heads // GROUP, n, LANES), f32),
            ],
            read,
            decay,
            step,
        ),
        after=(right_own,),
    )
    earlies = []
    for i in range(span - 1):
        leaving = early_term
        if i:
            ((leaving,),) = run(
                job(onward_kernel, [half_shape], early_term, early_decay, *earlies)
            )
        earlies.append(over_chips(leaving, (chips - 1 - i, chips - 2 - i)))
    ((right_term, right_decay),) = run(
        chip_job(False, right_own, right_near), after=(early_term,)
    )
    rights = [over_chips(right_term, (chips - 1, chips - 2))]
    got = over_cores(held)
    ((held,),) = run(
        job(
            pair_kernel,
            [sds((chips, 2, *local.shape), bf16)],
            held,
            got,
            scalars=(chip, core),
        ),
        after=(right_term,),
    )
    held = held.reshape(-1, state)
    (shares,) = run(
        job(share_kernel, [sds((2 * share, n), bf16)] * dp_count, hidden, held, scalars=(dp,))
    )
    shared = [shares[0]] + [over_dp(shares[k], k) for k in range(1, dp_count)]
    ((mix_f,),) = run(
        job(part(mix_kernel, True, [1]), [sds((n, n), f32)], gf, inner, rows[CUM2], cols),
        after=(right_term,),
    )
    right_far = over_cores(right_own)
    ((leaving,),) = run(
        job(onward_kernel, [half_shape], right_term, right_decay, *rights),
        after=(mix_f, right_far, *shared[1:4]),
    )
    rights.append(over_chips(leaving, (chips - 2, chips - 3)))

    ((left_own, *sends),) = run(
        part_job(None, flips, read_t, rows[BACK_WEIGHT]), after=(leaving,), flops=COSTLY
    )
    left_near = [over_cores(send) for send in sends]
    lefts = []
    for i in range(span - 1):
        early = [] if i else [early_term, early_decay, *earlies]
        shapes = [half_shape] * (1 if i else 2)
        (leaving, *middle), = run(
            job(
                part(left_kernel, len(early)),
                shapes,
                left_own,
                *left_near,
                *early,
                *lefts,
                scalars=(core, chip == span),
            )
        )
        lefts += middle
        lefts.append(over_chips(leaving, (i, i + 1), (span + i, span + i + 1)))
    left_far = over_cores(left_own)
    for i in range(2, chips - 1):
        ((leaving,),) = run(
            job(onward_kernel, [half_shape], right_term, right_decay, *rights),
        )
        rights.append(over_chips(leaving, (chips - 1 - i, chips - 2 - i)))
    ((mix_b,),) = run(
        job(
            part(mix_kernel, False, [len(flips)]),
            [sds((n, n), f32)],
            *flips,
            inner,
            rows[EXCLR2],
            cols,
        ),
        after=(leaving,),
    )
    ((halves,),) = run(
        job(part(halves_kernel, len(rights)), [sds((state, width), bf16)], *rights, *lefts),
        after=(left_far, mix_b, *shared[4:]),
    )
    swapped = over_cores(halves)

    ((right_own_in, left_own_in, own_write),) = run(
        job(
            own_kernel,
            [half_shape, half_shape, sds((n, state), f32)],
            inner,
            halves,
            rows,
            mix_f,
            mix_b,
            read,
            read_r,
            *right_near,
            *left_near,
            scalars=(core,),
        )
    )
    ((right_rest_in, left_rest_in, grad_write),) = run(
        job(
            write_kernel,
            [half_shape, half_shape, sds((n, state), bf16)],
            inner,
            swapped,
            rows,
            own_write,
            right_far,
            left_far,
            scalars=(core,),
        )
    )

    writes = [grad_write] + [over_dp(grad_write, k) for k in range(1, dp_count)]
    ((weight,),) = run(
        job(gather_kernel, [sds((dp_count, share, state), bf16)], *shared, scalars=(dp,)),
        after=(grad_write,),
    )
    weight = weight.reshape(-1, state)
    write = jnp.dot(hidden, weight, preferred_element_type=f32).astype(bf16)
    entering = (right_own_in, right_rest_in, left_own_in, left_rest_in)
    inner_arrays = (gf, *entering, rows, cols, write, read, read_r, *flips)
    half_inner = run_on_half(part(inner_kernel, 0), 0, sds((n, width), bf16), core, inner_arrays, ())
    piece = share // ctx_count
    ((keep, give),) = run(
        job(
            product_kernel,
            [sds((chips, piece, state), f32), sds((chips, piece, state), bf16)],
            *shared,
            *writes,
            scalars=(core,),
        ),
        after=(half_inner,),
    )
    ((total, *dealt),) = run(
        job(
            deal_kernel,
            [sds((piece, state), f32)] + [sds((piece, state), bf16)] * (chips - 1),
            keep,
            over_cores(give),
            scalars=(chip,),
        )
    )
    for k in range(1, chips):
        total = total + lax.ppermute(dealt[k - 1], "ctx", xor_pairs(ctx_count, 2 * k)).astype(f32)
    grad_weight = total / (dp_count * ctx_count * n)

    grad_inner = run_on_half(
        part(inner_kernel, 1), 1, sds((n, width), bf16), core, inner_arrays, (half_inner,), tuple(dealt[:1])
    )
    grad_hidden = dot_nt(grad_write, weight).astype(bf16)
    return grad_inner[None], grad_hidden[None], grad_weight


def solution(mesh):
    in_specs = (
        P("dp", "ctx", None),
        P(("dp", "ctx"), None),
        P(("dp", "ctx")),
        P("dp", "ctx", None),
        P("dp", "ctx", None),
        P("dp", None, "ctx"),
        P("dp", None, "ctx"),
        P("dp", "ctx", None),
        P("dp", "ctx", None),
    )
    out_specs = (P("dp", "ctx", None), P("dp", "ctx", None), P(("dp", "ctx"), None))
    return jax.shard_map(shards, mesh=mesh, in_specs=in_specs, out_specs=out_specs, check_vma=False)
```

```python
import functools
import itertools

import jax
import jax.numpy as jnp
from jax import lax
from jax.experimental import pallas as pl
from jax.experimental.pallas import tpu as pltpu
from jax.sharding import PartitionSpec as P

BLOCK = 128
LANES = 128
GROUP = 8
LOG2E = 1.4426950408889634
LOW = -1e30
EXACT = lax.Precision.HIGHEST
VMEM_BYTES = 9 * 1024 * 1024
CUT = 1024
PIECES = 2

f32 = jnp.float32
bf16 = jnp.bfloat16

CUM2, EXCLR2, FWD_EDGE, BACK_EDGE, STEP = range(5)
C_MIX_FWD, C_MIX_BACK, C_CUM2, C_EXCL2 = range(4)


def sds(shape, dtype):
    return jax.ShapeDtypeStruct(shape, dtype)


def job(body, outs, *arrays, scalars=()):
    return body, outs, arrays, [jnp.reshape(s, (1,)).astype(jnp.int32) for s in scalars]


def run(*jobs, after=(), flops=0):
    vmem = pl.BlockSpec(memory_space=pltpu.VMEM)
    smem = pl.BlockSpec(memory_space=pltpu.SMEM)
    ins, specs, outs, calls = [], [], [], []
    for body, job_outs, arrays, scalars in jobs:
        calls.append((body, len(ins), len(scalars) + len(arrays), len(outs), len(job_outs)))
        ins += [*scalars, *arrays]
        specs += [smem] * len(scalars) + [vmem] * len(arrays)
        outs += job_outs
    lead = len(ins)
    if after:
        ins[-1] = lax.optimization_barrier((ins[-1], *after))[0]

    def kernel(*refs):
        for body, i, ni, o, no in calls:
            body(*refs[i : i + ni], *refs[lead + o : lead + o + no])

    got = pl.pallas_call(
        kernel,
        out_shape=outs,
        in_specs=specs,
        out_specs=[vmem] * len(outs),
        compiler_params=pltpu.CompilerParams(vmem_limit_bytes=VMEM_BYTES),
        cost_estimate=pl.CostEstimate(flops=flops, transcendentals=0, bytes_accessed=flops // 250),
    )(*ins)
    return [list(got[o : o + no]) for _, _, _, o, no in calls]


def run_on_half(body, side, shape, scalar, arrays, before, after=()):
    vmem = pl.BlockSpec(memory_space=pltpu.VMEM)
    smem = pl.BlockSpec(memory_space=pltpu.SMEM)
    anywhere = pl.BlockSpec(memory_space=pl.ANY)
    rest = [*before]
    if after:
        arrays = [*arrays[:-1], lax.optimization_barrier((arrays[-1], *after))[0]]

    def kernel(*refs):
        body(*refs[: len(arrays) + 1], refs[-1])

    return pl.pallas_call(
        kernel,
        grid=(1,),
        out_shape=shape,
        in_specs=[smem] + [vmem] * len(arrays) + [anywhere] * len(rest),
        out_specs=pl.BlockSpec((shape.shape[0], shape.shape[1] // 2), lambda i: (0, side)),
        input_output_aliases={len(arrays) + 1: 0} if before else {},
        compiler_params=pltpu.CompilerParams(vmem_limit_bytes=VMEM_BYTES),
        cost_estimate=pl.CostEstimate(flops=0, transcendentals=0, bytes_accessed=0),
    )(jnp.reshape(scalar, (1,)).astype(jnp.int32), *arrays, *rest)


def iotas(shape):
    return lax.broadcasted_iota(jnp.int32, shape, 0), lax.broadcasted_iota(jnp.int32, shape, 1)


def dot_nt(a, b):
    return lax.dot_general(a, b, (((1,), (1,)), ((), ())), preferred_element_type=f32)


def dot_tn(a, b):
    return lax.dot_general(a, b, (((0,), (0,)), ((), ())), preferred_element_type=f32)


def spread(rows, width):
    high = rows.astype(bf16).astype(f32)
    both = jnp.concatenate([high, rows - high], axis=0).astype(bf16)
    r, c = iotas((2 * GROUP, GROUP * width))
    pick = (r % GROUP == c // width).astype(f32).astype(bf16)
    return dot_tn(both, pick)


def tables_kernel(read_ref, decay_ref, step_ref, readr_ref, rows_ref, cols_ref):
    decay = decay_ref[...]
    heads, n = decay.shape
    r, c = iotas((n, n))
    upto = (r <= c).astype(f32)
    flip = (r + c == n - 1).astype(f32)
    readr_ref[...] = jnp.dot(
        flip.astype(bf16), read_ref[...], preferred_element_type=f32
    ).astype(bf16)
    cum = jnp.dot(decay, upto, precision=EXACT, preferred_element_type=f32)
    decay_r = jnp.dot(decay, flip, precision=EXACT, preferred_element_type=f32)
    cum_r = jnp.dot(decay_r, upto, precision=EXACT, preferred_element_type=f32)
    end = cum[:, n - 1 :]
    excl = cum - decay
    step = step_ref[...]
    log_step = jnp.log(step) * LOG2E
    cum2 = cum * LOG2E
    excl2 = excl * LOG2E
    rows_ref[CUM2] = cum2
    rows_ref[EXCLR2] = (end - cum_r) * LOG2E
    rows_ref[FWD_EDGE] = step * jnp.exp(end - cum)
    rows_ref[BACK_EDGE] = step * jnp.exp(excl)
    rows_ref[STEP] = step
    planes = (cum2 - log_step, excl2 + log_step, cum2, excl2)
    rest = jnp.zeros((LANES - GROUP * len(planes), n), f32)
    for g in range(heads // GROUP):
        part = [p[g * GROUP : (g + 1) * GROUP] for p in planes]
        cols_ref[g] = jnp.concatenate(part + [rest], axis=0).T


def columns(refs, at, count, value=None):
    for ref in refs:
        if at < ref.shape[1]:
            if value is None:
                return ref[:, at : at + count]
            ref[:, at : at + count] = value
            return None
        at -= ref.shape[1]


def summed(lists, at, count):
    total = columns(lists[0], at, count)
    for refs in lists[1:]:
        total = total + columns(refs, at, count)
    return total


def split(refs, counts):
    lists = []
    for count in counts:
        lists.append(refs[:count])
        refs = refs[count:]
    return lists, refs


def part_kernel(backward, count, core_ref, *refs):
    g_refs, (read_ref, decay_ref, own_ref, *send_refs) = refs[:count], refs[count:]
    heads, n = decay_ref.shape
    width = sum(ref.shape[1] for ref in g_refs) // heads
    step = GROUP * width
    r, c = iotas((n, n))
    order = ((r + c == n - 1) if backward else (r == c)).astype(f32)
    upto = (r <= c).astype(f32)
    read_t = dot_tn(read_ref[...].astype(bf16), order.astype(bf16)).astype(bf16)
    decay = decay_ref[...]
    if backward:
        decay = jnp.dot(decay, order, precision=EXACT, preferred_element_type=f32)
    weight = jnp.exp(jnp.dot(decay, upto, precision=EXACT, preferred_element_type=f32))
    state = read_t.shape[0]
    groups = heads // GROUP
    tail_row, _ = iotas((16, step))
    low = core_ref[0] == 0

    def term_of(g):
        scale = spread(weight[g * GROUP : (g + 1) * GROUP], width)
        cotangent = columns(g_refs, g * step, step)
        scaled = (cotangent.astype(f32) * scale).astype(bf16)
        term = jnp.dot(read_t, scaled, preferred_element_type=f32)
        last = scale[n - 1 :]
        high = last.astype(bf16).astype(f32)
        tail = jnp.where(tail_row == 0, high, jnp.where(tail_row == 1, last - high, 0.0))
        return jnp.concatenate([term, tail], axis=0)

    for g in range(groups // 2):
        here = slice(g * step, (g + 1) * step)
        lower, upper = term_of(g), term_of(g + groups // 2)
        own_ref[:, here] = jnp.where(low, lower, upper).astype(bf16)
        sent = jnp.where(low, upper, lower).astype(bf16)
        columns(send_refs, g * step, step, sent)


WIDE = 512


def chip_terms(upward, core, own_ref, near_refs):
    state = own_ref.shape[0] - 16
    first = core == (0 if upward else 1)
    for c in range(own_ref.shape[1] // WIDE):
        here = slice(c * WIDE, (c + 1) * WIDE)
        own = own_ref[:, here].astype(f32)
        other = columns(near_refs, c * WIDE, WIDE).astype(f32)
        own_term, other_term = own[:state], other[:state]
        own_decay = own[state : state + 1] + own[state + 1 : state + 2]
        other_decay = other[state : state + 1] + other[state + 1 : state + 2]
        later = jnp.where(first, other_decay, own_decay)
        term = jnp.where(first, other_term, own_term) + later * jnp.where(
            first, own_term, other_term
        )
        yield here, term, own_decay * other_decay


def chip_kernel(upward, core_ref, own_ref, *refs):
    *near_refs, term_ref, decay_ref = refs
    for here, term, decay in chip_terms(upward, core_ref[0], own_ref, near_refs):
        term_ref[:, here] = term.astype(bf16)
        decay_ref[:, here] = decay


def entered(refs, here):
    state = refs[0][:, here].astype(f32)
    for ref in refs[1:]:
        state = state + ref[:, here].astype(f32)
    return state


def onward_kernel(term_ref, decay_ref, *refs):
    *entering, out_ref = refs
    for c in range(out_ref.shape[1] // WIDE):
        here = slice(c * WIDE, (c + 1) * WIDE)
        out_ref[:, here] = (
            term_ref[:, here].astype(f32) + decay_ref[:, here] * entered(entering, here)
        ).astype(bf16)


def middle_kernel(flag_ref, term_ref, decay_ref, *refs):
    *entering, out_ref = refs
    for c in range(out_ref.shape[1] // WIDE):
        here = slice(c * WIDE, (c + 1) * WIDE)
        leaving = term_ref[:, here].astype(f32)
        if entering:
            leaving = leaving + decay_ref[:, here] * entered(entering, here)
        out_ref[:, here] = jnp.where(flag_ref[0] == 1, leaving, 0.0).astype(bf16)


def left_kernel(count, core_ref, flag_ref, own_ref, *refs):
    near_refs, early, refs = refs[:PIECES], refs[PIECES : PIECES + count], refs[PIECES + count :]
    if early:
        out_ref, middle_ref = refs
        middle_kernel(flag_ref, *early, middle_ref)
        entering = [middle_ref]
    else:
        *entering, out_ref = refs
    for here, term, decay in chip_terms(True, core_ref[0], own_ref, near_refs):
        out_ref[:, here] = (term + decay * entered(entering, here)).astype(bf16)


def halves_kernel(count, *refs):
    rights, lefts, out_ref = refs[:count], refs[count:-1], refs[-1]
    half = out_ref.shape[1] // 2
    for c in range(half // WIDE):
        here = slice(c * WIDE, (c + 1) * WIDE)
        there = slice(half + c * WIDE, half + (c + 1) * WIDE)
        out_ref[:, here] = entered(rights, here).astype(bf16)
        out_ref[:, there] = entered(lefts, here).astype(bf16)


def mix_kernel(fwd, counts, *refs):
    lists, (inner_ref, row_ref, cols_ref, out_ref) = split(refs, counts)
    heads, n = row_ref.shape
    width = inner_ref.shape[1] // heads
    step = GROUP * width
    s, t = iotas((n, n))
    keep = (t >= s) if fwd else (t + s >= n - 1)
    low_half = t < width
    acc = jnp.zeros((n, n), f32)
    for g in range(heads // GROUP):
        rows = row_ref[g * GROUP : (g + 1) * GROUP]
        cols = cols_ref[g]
        for pair in range(GROUP // 2):
            at = g * step + pair * LANES
            inner = inner_ref[:, at : at + LANES].astype(f32)
            halves = jnp.concatenate(
                [jnp.where(low_half, inner, 0.0), jnp.where(low_half, 0.0, inner)], axis=0
            ).astype(bf16)
            dots = dot_nt(halves, summed(lists, at, LANES))
            for j in range(2):
                h = 2 * pair + j
                row = rows[h : h + 1]
                if fwd:
                    k = C_MIX_FWD * GROUP + h
                    power = row - cols[:, k : k + 1]
                else:
                    k = C_MIX_BACK * GROUP + h
                    power = cols[:, k : k + 1] - row
                decay = jnp.exp2(jnp.where(keep, power, LOW))
                acc = acc + decay * dots[j * n : (j + 1) * n]
    out_ref[...] = acc


def edge_terms(upward, own, core, inner_ref, half_ref, near_refs, far_ref, edge_ref, state_ref):
    heads, n = edge_ref.shape
    width = inner_ref.shape[1] // heads
    step = GROUP * width
    groups = heads // GROUP // 2
    first = core == (0 if upward else 1)
    rows = state_ref.shape[0]
    base = core if own else 1 - core
    at = groups * step if upward else 0
    acc = 0.0
    for g in range(groups):
        here = pl.ds(pl.multiple_of((base * groups + g) * step, step), step)
        heads_here = pl.ds(pl.multiple_of((base * groups + g) * GROUP, GROUP), GROUP)
        whole = half_ref[:, at + g * step : at + (g + 1) * step].astype(f32)
        other = columns(near_refs, g * step, step) if own else far_ref[:, g * step : (g + 1) * step]
        other = other.astype(f32)
        decay = other[rows : rows + 1] + other[rows + 1 : rows + 2]
        entering = jnp.where(first, whole, other[:rows] + decay * whole).astype(bf16)
        state_ref[:, g * step : (g + 1) * step] = entering
        scaled = inner_ref[:, here].astype(f32) * spread(edge_ref[heads_here], width)
        acc = acc + dot_nt(scaled.astype(bf16), entering)
    return acc


def own_kernel(
    core_ref, inner_ref, halves_ref, rows_ref, mixf_ref, mixb_ref, read_ref, readr_ref, *refs
):
    right_refs, left_refs = refs[:PIECES], refs[PIECES : 2 * PIECES]
    right_ref, left_ref, out_ref = refs[2 * PIECES :]
    acc = jnp.dot(mixf_ref[...].astype(bf16), read_ref[...], preferred_element_type=f32)
    acc = acc + jnp.dot(mixb_ref[...].astype(bf16), readr_ref[...], preferred_element_type=f32)
    for upward, near, plane, state_ref in (
        (False, right_refs, FWD_EDGE, right_ref),
        (True, left_refs, BACK_EDGE, left_ref),
    ):
        acc = acc + edge_terms(
            upward, True, core_ref[0], inner_ref, halves_ref, near, None, rows_ref.at[plane], state_ref
        )
    out_ref[...] = acc


def write_kernel(
    core_ref, inner_ref, swapped_ref, rows_ref, acc_ref, right_far_ref, left_far_ref, *refs
):
    right_ref, left_ref, out_ref = refs
    acc = acc_ref[...]
    for upward, far, plane, state_ref in (
        (False, right_far_ref, FWD_EDGE, right_ref),
        (True, left_far_ref, BACK_EDGE, left_ref),
    ):
        acc = acc + edge_terms(
            upward, False, core_ref[0], inner_ref, swapped_ref, None, far, rows_ref.at[plane], state_ref
        )
    out_ref[...] = acc.astype(bf16)


def share_kernel(dp_ref, hidden_ref, weight_ref, *out_refs):
    share = weight_ref.shape[0]
    for k, out_ref in enumerate(out_refs):
        for c in range(share // LANES):
            at = pl.multiple_of((dp_ref[0] ^ k) * share + c * LANES, LANES)
            out_ref[c * LANES : (c + 1) * LANES] = (
                hidden_ref[:, pl.ds(at, LANES)].astype(f32).T.astype(bf16)
            )
        out_ref[share:] = weight_ref[...]


def product_kernel(core_ref, *refs):
    count = (len(refs) - 2) // 2
    hidden_refs, write_refs = refs[:count], refs[count : 2 * count]
    keep_ref, give_ref = refs[2 * count :]
    chips, piece, _ = keep_ref.shape
    writes = [w[...] for w in write_refs]
    for which, out_ref in ((core_ref[0], keep_ref), (1 - core_ref[0], give_ref)):
        for chip in range(chips):
            rows = pl.ds(pl.multiple_of((2 * chip + which) * piece, piece), piece)
            total = jnp.dot(hidden_refs[0][rows], writes[0], preferred_element_type=f32)
            for k in range(1, count):
                total = total + jnp.dot(hidden_refs[k][rows], writes[k], preferred_element_type=f32)
            out_ref[chip] = total.astype(out_ref.dtype)


def deal_kernel(chip_ref, keep_ref, got_ref, own_ref, *out_refs):
    chip = chip_ref[0]
    own_ref[...] = keep_ref[chip] + got_ref[chip].astype(f32)
    for k, out_ref in enumerate(out_refs, 1):
        out_ref[...] = (keep_ref[chip ^ k] + got_ref[chip ^ k].astype(f32)).astype(bf16)


def cut_kernel(start, array_ref, out_ref):
    out_ref[...] = array_ref[:, start : start + out_ref.shape[1]]


def stack_kernel(*refs):
    *arrays, out_ref = refs
    for k, ref in enumerate(arrays):
        out_ref[k] = ref[...].astype(bf16)


def pair_kernel(chip_ref, core_ref, held_ref, got_ref, out_ref):
    chip, core = chip_ref[0], core_ref[0]
    chips = held_ref.shape[0]
    for k in range(chips):
        held_core = core if k < chips - 1 else 1 - core
        out_ref[chip ^ k, held_core] = held_ref[k]
        out_ref[chip ^ k, 1 - held_core] = got_ref[k]


def gather_kernel(index_ref, *refs):
    *arrays, out_ref = refs
    rows = out_ref.shape[1]
    for k, ref in enumerate(arrays):
        out_ref[index_ref[0] ^ k] = ref[ref.shape[0] - rows :]


def inner_kernel(
    side, core_ref, gf_ref, right_own_ref, right_rest_ref, left_own_ref, left_rest_ref, *refs
):
    rows_ref, cols_ref, write_ref, read_ref, readr_ref, *gb_refs, out_ref = refs
    own_side = core_ref[0] == side
    _, heads, n = rows_ref.shape
    width = gf_ref.shape[1] // heads
    step = GROUP * width
    half = heads // GROUP // 2
    write = write_ref[...]
    kernel_f = dot_nt(write, read_ref[...])
    kernel_b = dot_nt(write, readr_ref[...])
    s, t = iotas((n, n))
    low_half = t < width

    for g in range(side * half, (side + 1) * half):
        at = g * step
        own = slice(g * GROUP, (g + 1) * GROUP)
        half_at = at - side * half * step
        there = slice(half_at, half_at + step)
        cols = cols_ref[g]
        right = jnp.where(own_side, right_own_ref[:, there], right_rest_ref[:, there])
        left = jnp.where(own_side, left_own_ref[:, there], left_rest_ref[:, there])
        cum2 = rows_ref[CUM2, own]
        exclr2 = rows_ref[EXCLR2, own]
        step_e = spread(rows_ref[STEP, own], width)
        edges = spread(rows_ref[FWD_EDGE, own], width) * jnp.dot(
            write, right, preferred_element_type=f32
        )
        edges = edges + spread(rows_ref[BACK_EDGE, own], width) * jnp.dot(
            write, left, preferred_element_type=f32
        )
        for pair in range(GROUP // 2):
            mixes = []
            for j in range(2):
                h = 2 * pair + j
                kf = C_CUM2 * GROUP + h
                kb = C_EXCL2 * GROUP + h
                pf = cum2[h : h + 1] - cols[:, kf : kf + 1]
                pb = cols[:, kb : kb + 1] - exclr2[h : h + 1]
                mf = jnp.exp2(jnp.where(t >= s, pf, LOW)) * kernel_f
                mb = jnp.exp2(jnp.where(t + s >= n - 1, pb, LOW)) * kernel_b
                mixes.append(jnp.concatenate([mf, mb], axis=1))
            here = at + pair * LANES
            both = jnp.concatenate(
                [gf_ref[:, here : here + LANES], columns(gb_refs, here, LANES)], axis=0
            )
            got = jnp.dot(
                jnp.concatenate(mixes, axis=0).astype(bf16), both, preferred_element_type=f32
            )
            intra = jnp.where(low_half, got[:n], got[n:])
            mine = slice(pair * LANES, (pair + 1) * LANES)
            into = (g - side * half) * step + pair * LANES
            out_ref[:, into : into + LANES] = (step_e[:, mine] * intra + edges[:, mine]).astype(
                bf16
            )


def xor_pairs(count, k):
    return [(i, i ^ k) for i in range(count)]


def chip_pairs(moves):
    return [(2 * a + i, 2 * b + i) for a, b in moves for i in range(2)]


def shards(
    hidden_in,
    write_weight,
    shard_scale,
    inner_acts,
    read_proj,
    step_size,
    log_decay,
    grad_fwd,
    grad_rev,
):
    ctx_count = lax.axis_size("ctx")
    dp_count = lax.axis_size("dp")
    ctx = lax.axis_index("ctx")
    dp = lax.axis_index("dp")
    core, chip = ctx % 2, ctx // 2
    chips = ctx_count // 2
    span = chips // 2
    hidden = hidden_in[0]
    inner = inner_acts[0]
    read = read_proj[0]
    step = step_size[0]
    decay = log_decay[0]
    gf = grad_fwd[0]
    gr = grad_rev[0]
    n, width = inner.shape
    heads = decay.shape[0]
    state = read.shape[1]
    half = width // 2
    share = hidden.shape[1] // dp_count
    part = functools.partial
    part_shapes = [sds((state + 16, half), bf16)]
    part_shapes += [sds((state + 16, half // PIECES), bf16)] * PIECES
    half_shape = sds((state, half), bf16)
    chip_shapes = [half_shape, sds((1, half), f32)]

    def over_cores(array):
        return lax.ppermute(array, "ctx", xor_pairs(ctx_count, 1))

    def over_chips(array, *moves):
        return lax.ppermute(array, "ctx", chip_pairs(moves))

    def over_dp(array, k):
        return lax.ppermute(array, "dp", xor_pairs(dp_count, k))

    def flip(piece):
        return lax.ppermute(piece, "ctx", [(i, ctx_count - 1 - i) for i in range(ctx_count)])

    local = (write_weight.astype(f32) * shard_scale[0]).astype(bf16)
    mirrored = flip(jnp.concatenate([read.astype(f32), decay, local.astype(f32)], axis=0))
    weights = [local] + [
        lax.ppermute(local, "ctx", xor_pairs(ctx_count, 2 * k)) for k in range(1, chips - 1)
    ]
    cuts = [(0, CUT), (CUT, width)]
    pieces = run(
        *(job(part(cut_kernel, a), [sds((n, b - a), bf16)], gr) for a, b in cuts),
        after=(mirrored, *weights),
    )
    flips = [flip(pieces[0][0])]
    flips.append(flip(lax.optimization_barrier((pieces[1][0], flips[0]))[0]))

    def part_job(backward, pieces, *arrays):
        body = part(part_kernel, backward, len(pieces))
        return job(body, part_shapes, *pieces, *arrays, scalars=(core,))

    def chip_job(upward, own, near):
        return job(part(chip_kernel, upward), chip_shapes, own, *near, scalars=(core,))

    ((held,),) = run(
        job(stack_kernel, [sds((chips, *local.shape), bf16)], *weights, mirrored[n + heads :])
    )
    ((early_own, *sends),) = run(
        part_job(True, [gr], mirrored[:n], mirrored[n : n + heads]), after=(held,)
    )
    early_near = [over_cores(send) for send in sends]
    ((right_own, *sends),) = run(part_job(False, [gf], read, decay))
    right_near = [over_cores(send) for send in sends]
    (early_term, early_decay), (read_r, rows, cols) = run(
        chip_job(False, early_own, early_near),
        job(
            tables_kernel,
            [
                sds((n, state), bf16),
                sds((5, heads, n), f32),
                sds((heads // GROUP, n, LANES), f32),
            ],
            read,
            decay,
            step,
        ),
        after=(right_own,),
    )
    earlies = []
    for i in range(span - 1):
        leaving = early_term
        if i:
            ((leaving,),) = run(
                job(onward_kernel, [half_shape], early_term, early_decay, *earlies)
            )
        earlies.append(over_chips(leaving, (chips - 1 - i, chips - 2 - i)))
    ((right_term, right_decay),) = run(
        chip_job(False, right_own, right_near), after=(early_term,)
    )
    rights = [over_chips(right_term, (chips - 1, chips - 2))]
    got = over_cores(held)
    ((held,),) = run(
        job(
            pair_kernel,
            [sds((chips, 2, *local.shape), bf16)],
            held,
            got,
            scalars=(chip, core),
        ),
        after=(right_term,),
    )
    held = held.reshape(-1, state)
    (shares,) = run(
        job(share_kernel, [sds((2 * share, n), bf16)] * dp_count, hidden, held, scalars=(dp,))
    )
    shared = [shares[0]] + [over_dp(shares[k], k) for k in range(1, dp_count)]
    ((mix_f,),) = run(
        job(part(mix_kernel, True, [1]), [sds((n, n), f32)], gf, inner, rows[CUM2], cols),
        after=(right_term,),
    )
    right_far = over_cores(right_own)
    ((leaving,),) = run(
        job(onward_kernel, [half_shape], right_term, right_decay, *rights),
        after=(mix_f, right_far, *shared[1:4]),
    )
    rights.append(over_chips(leaving, (chips - 2, chips - 3)))

    ((left_own, *sends),) = run(part_job(True, flips, read, decay), after=(leaving,))
    left_near = [over_cores(send) for send in sends]
    lefts = []
    for i in range(span - 1):
        early = [] if i else [early_term, early_decay, *earlies]
        shapes = [half_shape] * (1 if i else 2)
        (leaving, *middle), = run(
            job(
                part(left_kernel, len(early)),
                shapes,
                left_own,
                *left_near,
                *early,
                *lefts,
                scalars=(core, chip == span),
            )
        )
        lefts += middle
        lefts.append(over_chips(leaving, (i, i + 1), (span + i, span + i + 1)))
    left_far = over_cores(left_own)
    for i in range(2, chips - 1):
        ((leaving,),) = run(
            job(onward_kernel, [half_shape], right_term, right_decay, *rights),
        )
        rights.append(over_chips(leaving, (chips - 1 - i, chips - 2 - i)))
    ((mix_b,),) = run(
        job(
            part(mix_kernel, False, [len(flips)]),
            [sds((n, n), f32)],
            *flips,
            inner,
            rows[EXCLR2],
            cols,
        ),
        after=(leaving,),
    )
    ((halves,),) = run(
        job(part(halves_kernel, len(rights)), [sds((state, width), bf16)], *rights, *lefts),
        after=(left_far, mix_b, *shared[4:]),
    )
    swapped = over_cores(halves)

    ((right_own_in, left_own_in, own_write),) = run(
        job(
            own_kernel,
            [half_shape, half_shape, sds((n, state), f32)],
            inner,
            halves,
            rows,
            mix_f,
            mix_b,
            read,
            read_r,
            *right_near,
            *left_near,
            scalars=(core,),
        )
    )
    ((right_rest_in, left_rest_in, grad_write),) = run(
        job(
            write_kernel,
            [half_shape, half_shape, sds((n, state), bf16)],
            inner,
            swapped,
            rows,
            own_write,
            right_far,
            left_far,
            scalars=(core,),
        )
    )

    writes = [grad_write] + [over_dp(grad_write, k) for k in range(1, dp_count)]
    ((weight,),) = run(
        job(gather_kernel, [sds((dp_count, share, state), bf16)], *shared, scalars=(dp,)),
        after=(grad_write,),
    )
    weight = weight.reshape(-1, state)
    write = jnp.dot(hidden, weight, preferred_element_type=f32).astype(bf16)
    entering = (right_own_in, right_rest_in, left_own_in, left_rest_in)
    inner_arrays = (gf, *entering, rows, cols, write, read, read_r, *flips)
    half_inner = run_on_half(part(inner_kernel, 0), 0, sds((n, width), bf16), core, inner_arrays, ())
    piece = share // ctx_count
    ((keep, give),) = run(
        job(
            product_kernel,
            [sds((chips, piece, state), f32), sds((chips, piece, state), bf16)],
            *shared,
            *writes,
            scalars=(core,),
        ),
        after=(half_inner,),
    )
    ready_write = lax.optimization_barrier((grad_write, give))[0]
    grad_hidden = dot_nt(ready_write, weight).astype(bf16)
    ((total, *dealt),) = run(
        job(
            deal_kernel,
            [sds((piece, state), f32)] + [sds((piece, state), bf16)] * (chips - 1),
            keep,
            over_cores(give),
            scalars=(chip,),
        ),
        after=(grad_hidden,),
    )
    for k in range(1, chips):
        total = total + lax.ppermute(dealt[k - 1], "ctx", xor_pairs(ctx_count, 2 * k)).astype(f32)
    grad_weight = total / (dp_count * ctx_count * n)

    grad_inner = run_on_half(
        part(inner_kernel, 1), 1, sds((n, width), bf16), core, inner_arrays, (half_inner,), tuple(dealt[:1])
    )
    return grad_inner[None], grad_hidden[None], grad_weight


def solution(mesh):
    in_specs = (
        P("dp", "ctx", None),
        P(("dp", "ctx"), None),
        P(("dp", "ctx")),
        P("dp", "ctx", None),
        P("dp", "ctx", None),
        P("dp", None, "ctx"),
        P("dp", None, "ctx"),
        P("dp", "ctx", None),
        P("dp", "ctx", None),
    )
    out_specs = (P("dp", "ctx", None), P("dp", "ctx", None), P(("dp", "ctx"), None))
    return jax.shard_map(shards, mesh=mesh, in_specs=in_specs, out_specs=out_specs, check_vma=False)
```
